256 devices in a mesh: rep: 8 (over x, y_lo), tp: 16 (over z, core), tail: 2 (over y_hi).
Axes of the slice: x: 4, y: 4 (y_hi: 2, y_lo: 2; y = y_hi * 2 + y_lo), z: 8, core: 2. Of those that a mesh axis runs over, the one named last changes fastest.
Arguments:
- tokens: bfloat16 [2048, 5120], P('rep', ('tp', 'tail')), may hold values from -6 to 6
- w_gate: bfloat16 [5120, 12800], P(None, ('tp', 'tail')), may hold values from -0.15625 to 0.15625
- w_up: bfloat16 [5120, 12800], P(None, ('tp', 'tail')), may hold values from -0.078125 to 0.078125
- hidden_grad: bfloat16 [2048, 12800], P('rep', ('tp', 'tail')), may hold values from -6 to 6
- kv_pool: bfloat16 [8192, 16, 1024], P(('rep', 'tp', 'tail')), may hold values from -6 to 6
- block_table: int32 [32, 256], P(('rep', 'tail'), 'tp'), may hold values from 0 to 31, as said below
- tail_len: int32 [32], replicated, may hold values from 1 to 4096, 32768 in all
- tail_owner: int32 [32, 1], replicated, may hold values from 0 to 1; in each aligned block of 2 rows (0 to 1, 2 to 3, ...) at most 2 rows name the same one
- new_queries: bfloat16 [32, 2, 4096], P(('rep', 'tail')), may hold values from -360 to 360
- new_kv: bfloat16 [32, 2, 1024], P(('rep', 'tail')), may hold values from -6 to 6
Outputs:
- input_grad: bfloat16 [2048, 5120], P('rep', ('tp', 'tail'))
- grad_gate: bfloat16 [5120, 12800], P('rep', ('tp', 'tail'))
- grad_up: bfloat16 [5120, 12800], P('rep', ('tp', 'tail'))
- tail_attn: bfloat16 [64, 2, 4096], P(('rep', 'tail'), None, 'tp')
The draws below stay inside these ranges and needn't reach their ends.
Inputs may be any that keep to these rules, and one draw needn't show every extreme that they name: `tail_owner`: within the 2 tails of one home (aligned blocks of rows), no owner is named more than 2 times; in some block an owner is named exactly 2 times. `block_table`: the entries of one home and one index of tp are a permutation of 0 to 31; blocks beyond a tail's length point at pages too.
All inputs are finite; a program needn't handle non-finite values.
Results may differ from the reference program's by a relative error of at most 0.0049.
Values may be sent and summed in bfloat16 or wider, within the bound.
A program may use at most 128 MiB of HBM per device.

```python
import math
import jax
import jax.numpy as jnp
import numpy as np
from jax import lax

D = 5120
FF = 12800
QH = 32
KVH = 4
HD = 128
STEPS = 2
PAGE = 16
TAIL_DEV = 2
CPD = 256
KVF = 1024
QF = 4096
BLOCK_DEV = 16
POOL_DEV = 32
BLOCKS = 256
CAP = 4096
TAILS = 32
MOST = 2
SLOTS = 64
POOL = 8192
TOKENS = 2048
N_REP = 8
N_TP = 16
N_TAIL = 2


def draw_block_table(key, part):
    key = jax.random.fold_in(key, 5)
    groups = N_REP * N_TAIL * N_TP
    subkeys = jax.random.split(key, groups)
    orders = jax.vmap(lambda single: jax.random.permutation(single, TAIL_DEV * BLOCK_DEV))(subkeys)
    orders = orders.reshape(N_REP * N_TAIL, N_TP, TAIL_DEV, BLOCK_DEV)
    return jnp.transpose(orders, (0, 2, 1, 3)).reshape(TAILS, BLOCKS).astype(jnp.int32)


def draw_new_queries(key, part):
    key = jax.random.fold_in(key, 11)
    noise_key = jax.random.fold_in(key, 0)
    values = jnp.clip(jax.random.normal(noise_key, (TAILS, STEPS, QH, HD), jnp.float32), -6.0, 6.0)
    return values.reshape(TAILS, STEPS, QH * HD).astype(jnp.bfloat16)


def with_spikes(result, key, source, target, parts, factor):
    owner, partner = [(jnp.arange(result.shape[dim]) // (result.shape[dim] // parts)).reshape([-1 if axis == dim else 1 for axis in range(result.ndim)]) for dim in (source, target)]
    chosen = jax.random.permutation(key, parts)[partner]
    strong = (owner == chosen) | (owner == (partner + parts // 2) % parts)
    return jnp.where(strong, factor * result, result)


def shard_levels(rng, dims, cuts, smallest, high):
    def one(dim, parts):
        steps = jax.random.uniform(jax.random.fold_in(jax.random.fold_in(rng, 6), dim), (parts,), jnp.float32, smallest / len(cuts), high / len(cuts))
        return jnp.repeat(jnp.exp(steps), dims[dim] // parts).reshape((-1,) + (1,) * (len(dims) - dim - 1))

    loudness = one(*cuts[0])
    for cut in cuts[1:]:
        loudness = loudness * one(*cut)
    return loudness


def length_profile(count, total, most, skew):
    loads = [(1 << 20) // math.isqrt(standing ** skew) + 1 for standing in range(2, count + 1)]
    rest, given = total - most - (count - 1), [1] * (count - 1)
    while rest > 0:
        candidates = [i for i in range(count - 1) if given[i] < most]
        whole, budget = sum([loads[i] for i in candidates]), rest
        for i in candidates:
            extra = min(most - given[i], max(1, budget * loads[i] // whole), rest)
            given[i] = given[i] + extra
            rest = rest - extra
    return np.array([most] + given)


def uneven(key, number_of, total, bound, lean):
    if number_of == 2:
        one = jax.random.randint(key, (), max(1, total - bound), min(bound, total - 1) + 1)
        return jnp.stack([one, total - one])
    sizes = jnp.asarray(length_profile(number_of, total, bound, lean), jnp.int32)
    pairs = (number_of - 1) // 2
    source_of, sink = sizes[1:1 + 2 * pairs:2], sizes[2:2 + 2 * pairs:2]
    margin = jnp.minimum(source_of - 1, bound - sink)
    moved = jax.random.randint(jax.random.fold_in(key, 1), (pairs,), 0, 1 << 20) % (margin + 1)
    sizes = sizes.at[1:1 + 2 * pairs:2].set(source_of - moved).at[2:2 + 2 * pairs:2].set(sink + moved)
    return sizes[jax.random.permutation(jax.random.fold_in(key, 2), number_of)]


def routed_block(own_key, own, number, rows, amount, top, most, lean):
    sequence = jax.random.permutation(own_key, amount)
    heavy_load, ordinary = load_shares(amount, rows * top, most, lean, True), load_shares(amount, rows * top, most, lean, False)
    places = jnp.arange(amount)

    def named(sizes, turn):
        used = int((sizes > 0).sum())
        fixed = max(1, used // 4)
        passed = fixed + (places - fixed + turn * (used - fixed)) % max(1, amount - fixed)
        return jnp.zeros((amount,), jnp.int32).at[sequence[jnp.where(places < fixed, places, passed)]].set(jnp.asarray(sizes, jnp.int32))

    sizes = jnp.where(number % 4 == 0, named(heavy_load, number // 4), named(ordinary, number - number // 4 - 1))
    mixed = jax.random.permutation(jax.random.fold_in(own, 3), amount)
    source_of, taker = mixed[0:amount // 2 * 2:2], mixed[1:amount // 2 * 2:2]
    room = jnp.minimum(sizes[source_of] - 1, most - sizes[taker]) // 2
    room = jnp.where((source_of == sequence[0]) | (taker == sequence[0]) | (sizes[taker] == 0), 0, jnp.maximum(room, 0))
    passed = jax.random.randint(jax.random.fold_in(own, 4), (amount // 2,), 0, 1 << 20) % (room + 1)
    sizes = sizes.at[source_of].add(-passed).at[taker].add(passed)
    members = jnp.searchsorted(jnp.cumsum(sizes), jnp.arange(rows * top), side="right").astype(jnp.int32)
    grid = members.reshape(top, rows).T
    grid = grid[jax.random.permutation(jax.random.fold_in(own, 1), rows)]
    turn = jax.random.randint(jax.random.fold_in(own, 2), (rows, 1), 0, top)
    return jnp.take_along_axis(grid, (jnp.arange(top)[None, :] + turn) % top, axis=1)


def load_shares(count, total, most, lean, full):
    loads = [(1 << 20) // math.isqrt(standing ** lean) + 1 for standing in range(1, count + 1)]
    largest = most if full else min(most, max(-(-total // count), total * loads[0] // sum(loads)))
    least = 1 if total - largest >= count - 1 else 0
    given, spare = [largest] + [least] * (count - 1), total - largest - least * (count - 1)
    while spare > 0:
        candidates = [i for i in range(1, count) if given[i] < largest] or [i for i in range(1, count) if given[i] < most]
        mass, budget = sum([loads[i] for i in candidates]), spare
        for i in candidates:
            extra = min(most - given[i], max(1, budget * loads[i] // mass), spare)
            given[i] = given[i] + extra
            spare = spare - extra
    return np.array(given)


def bell_draw(stream_key, dims, deviation, reach, cuts=(), kind=jnp.bfloat16):
    entries = deviation * jax.random.normal(stream_key, dims, jnp.float32)
    if cuts:
        entries = entries * shard_levels(stream_key, dims, cuts, -0.22, 0.18)
    return jnp.clip(entries, -reach, reach).astype(kind)


def noise_with(own_key, dims, width, bound, cuts, heavy, held_as=jnp.bfloat16):
    values = width * jax.random.normal(own_key, dims, jnp.float32)
    if cuts:
        values = values * shard_levels(own_key, dims, cuts, -0.22, 0.18)
    return jnp.clip(with_spikes(values, jax.random.fold_in(own_key, 3), *heavy), -bound, bound).astype(held_as)


def setup_inputs(seed: int = 0) -> dict:
    splits = jax.random.split(jax.random.key(seed), 11)
    tokens = noise_with(splits[0], (TOKENS, D), 1.0, 6.0, ((0, 8), (1, 32)), (0, 1, 32, 2.75))
    w_gate = noise_with(splits[1], (D, FF), D ** -0.5, 0.15625, ((1, 32),), (1, 0, 32, 2.75))
    w_up = bell_draw(splits[2], (D, FF), D ** -0.5, 0.078125, ((1, 32),))
    hidden_grad = bell_draw(splits[3], (TOKENS, FF), 1.0, 6.0, ((0, 8), (1, 32)))
    kv_pool = bell_draw(splits[4], (POOL, PAGE, KVF), 1.0, 6.0, ((0, 256),))
    block_table = draw_block_table(jax.random.fold_in(splits[10], 71), 0)
    tail_len = uneven(splits[6], TAILS, TAILS * CAP // 4, CAP, 2).astype(jnp.int32)
    tail_owner_keys = jax.random.split(jax.random.fold_in(splits[7], 1), TAILS // TAIL_DEV)
    tail_owner_turns = jax.random.permutation(jax.random.fold_in(splits[7], 3), TAILS // TAIL_DEV)
    tail_owner = jax.vmap(lambda own, number: routed_block(jax.random.fold_in(splits[7], 2), own, number, TAIL_DEV, N_TAIL, 1, MOST, 2))(tail_owner_keys, tail_owner_turns).reshape((TAILS, 1))
    new_queries = draw_new_queries(jax.random.fold_in(splits[10], 71), 0)
    new_kv = bell_draw(splits[9], (TAILS, STEPS, KVF), 1.0, 6.0, ((0, 16),))
    return dict(tokens=tokens, w_gate=w_gate, w_up=w_up, hidden_grad=hidden_grad, kv_pool=kv_pool, block_table=block_table, tail_len=tail_len, tail_owner=tail_owner, new_queries=new_queries, new_kv=new_kv)


MASK_VALUE = -1e30


def block_partials(queries, keys, values, is_live):
    scores = jnp.einsum("sgqd,bcgd->sgqbc", queries, keys.astype(jnp.float32)) * (HD ** -0.5)
    masked = jnp.where(is_live, scores, MASK_VALUE)
    block_max = jnp.max(masked, axis=-1)
    weights = jnp.where(is_live, jnp.exp(masked - block_max[..., None]), 0.0)
    block_sum = jnp.sum(weights, axis=-1)
    rounded = lax.optimization_barrier(weights.astype(jnp.bfloat16)).astype(jnp.float32)
    block_out = jnp.einsum("sgqbc,bcgd->sgqbd", rounded, values.astype(jnp.float32))
    return block_max, block_sum, block_out


def attend_tail(cached, length, queries, fresh_kv):
    split_kv = cached.reshape(N_TP, CPD, 2, KVH, HD)
    position = jnp.arange(N_TP * CPD, dtype=jnp.int32).reshape(N_TP, CPD)
    is_live = (position < length)[None, None, None, :, :]
    grouped = queries.reshape(STEPS, KVH, QH // KVH, HD).astype(jnp.float32)
    cache_max, cache_sum, cache_out = block_partials(grouped, split_kv[:, :, 0], split_kv[:, :, 1], is_live)
    fresh_split = fresh_kv.reshape(1, STEPS, 2, KVH, HD)
    causal = (jnp.arange(STEPS)[:, None] >= jnp.arange(STEPS)[None, :])[:, None, None, None, :]
    fresh_max, fresh_sum, fresh_out = block_partials(grouped, fresh_split[:, :, 0], fresh_split[:, :, 1], causal)
    all_max = jnp.concatenate([cache_max, fresh_max], axis=-1)
    all_sum = jnp.concatenate([cache_sum, fresh_sum], axis=-1)
    all_out = jnp.concatenate([cache_out, fresh_out], axis=-2)
    highest = jnp.max(all_max, axis=-1, keepdims=True)
    scaling = jnp.exp(all_max - highest)
    denominator = jnp.sum(scaling * all_sum, axis=-1)
    numerator = jnp.sum(scaling[..., None] * all_out, axis=-2)
    return (numerator / denominator[..., None]).reshape(STEPS, QF).astype(jnp.bfloat16)


def reference(tokens, w_gate, w_up, hidden_grad, kv_pool, block_table, tail_len, tail_owner, new_queries, new_kv):
    gate_pre = jnp.dot(tokens, w_gate, preferred_element_type=jnp.float32)
    up_pre = jnp.dot(tokens, w_up, preferred_element_type=jnp.float32)
    sigmoid_gate = jax.nn.sigmoid(gate_pre)
    grad_out = hidden_grad.astype(jnp.float32)
    act_gate = (grad_out * up_pre * sigmoid_gate * (1.0 + gate_pre * (1.0 - sigmoid_gate))).astype(jnp.bfloat16)
    act_up = (grad_out * gate_pre * sigmoid_gate).astype(jnp.bfloat16)
    input_grad = (jnp.dot(act_gate, w_gate.T, preferred_element_type=jnp.float32)
                  + jnp.dot(act_up, w_up.T, preferred_element_type=jnp.float32)).astype(jnp.bfloat16)
    grad_scale = TOKENS ** -0.5
    grad_gate = (jnp.dot(tokens.T, act_gate, preferred_element_type=jnp.float32) * grad_scale).astype(jnp.bfloat16)
    grad_up = (jnp.dot(tokens.T, act_up, preferred_element_type=jnp.float32) * grad_scale).astype(jnp.bfloat16)

    homes = N_REP * N_TAIL
    tail_ids = jnp.arange(TAILS, dtype=jnp.int32)
    home = tail_ids // TAIL_DEV
    block_ids = jnp.arange(BLOCKS, dtype=jnp.int32)
    shard = ((home // N_TAIL)[:, None] * N_TP + (block_ids // BLOCK_DEV)[None, :]) * N_TAIL + (home % N_TAIL)[:, None]
    page_ids = (shard * POOL_DEV + block_table).astype(jnp.int32)

    def one_tail(inputs):
        tail_pages, length, queries, fresh_kv = inputs
        cached = kv_pool[tail_pages].reshape(CAP, KVF)
        return attend_tail(cached, length, queries, fresh_kv)

    attended = lax.map(one_tail, (page_ids, tail_len, new_queries, new_kv))
    owners = tail_owner.reshape(homes, TAIL_DEV).astype(jnp.int32)
    onehot = (owners[:, :, None] == jnp.arange(N_TAIL, dtype=jnp.int32)[None, None, :]).astype(jnp.int32)
    rank_all = jnp.sum((jnp.cumsum(onehot, axis=1) - onehot) * onehot, axis=2)
    home_ids = jnp.arange(homes, dtype=jnp.int32)[:, None]
    replica = home_ids // N_TAIL
    source = home_ids % N_TAIL
    slot_ids = ((replica * N_TAIL + owners) * (2 * TAIL_DEV) + source * MOST + rank_all).reshape(TAILS).astype(jnp.int32)
    tail_attn = jnp.zeros((SLOTS, STEPS, QF), jnp.bfloat16).at[slot_ids].set(attended)
    return input_grad, grad_gate, grad_up, tail_attn
```

```python
import jax
import jax.numpy as jnp
from jax import lax
from jax.experimental import pallas as pl
from jax.experimental.pallas import tpu as pltpu
from jax.sharding import PartitionSpec as P

NR = 8
NZ = 8
NX = 4
NTP = 16
ROWS = 160
TOK = 256
HID = 400
LO = 208
KVH = 4
HD = 128
CPD = 256
POS = 512
MASK_VALUE = -1e30
SCALE = 2048 ** (-0.5)
F32 = jnp.float32
BF16 = jnp.bfloat16
NT = (((1,), (1,)), ((), ()))
MESH = pl.DeviceIdType.MESH
N_SEMS = 280

SCRATCH = dict(
    tok=pltpu.VMEM((TOK, ROWS), BF16),
    xt=pltpu.VMEM((NZ, 4, ROWS, TOK), BF16),
    yt=pltpu.VMEM((NR, 4, ROWS, TOK), BF16),
    wg=pltpu.VMEM((NZ, 2, 2 * ROWS, HID), BF16),
    wu=pltpu.VMEM((NZ, 2, 2 * ROWS, HID), BF16),
    hgrad=pltpu.VMEM((TOK, HID), BF16),
    hg=pltpu.VMEM((TOK, HID), F32),
    hu=pltpu.VMEM((TOK, HID), F32),
    ag=pltpu.VMEM((NR, HID, TOK), BF16),
    au=pltpu.VMEM((NR, HID, TOK), BF16),
    pf=pltpu.VMEM((NZ, 2, ROWS, TOK), F32),
    ss=pltpu.VMEM((NZ, 2, ROWS, TOK), BF16),
    sb=pltpu.VMEM((NZ, 2, ROWS, TOK), BF16),
    rs=pltpu.VMEM((14, ROWS, TOK), BF16),
    rb=pltpu.VMEM((14, ROWS, TOK), BF16),
    fin=pltpu.VMEM((2, ROWS, TOK), F32),
    ysend=pltpu.VMEM((ROWS, TOK), BF16),
    yrecv=pltpu.VMEM((ROWS, TOK), BF16),
    dg=pltpu.VMEM((2, 2 * ROWS, HID), F32),
    du=pltpu.VMEM((2, 2 * ROWS, HID), F32),
    kv=pltpu.VMEM((POS, 1024), BF16),
    qs=pltpu.VMEM((KVH, 32, HD), F32),
    kf=pltpu.VMEM((16, 1024), F32),
    ao=pltpu.VMEM((NTP, 24, HD), F32),
    ar=pltpu.VMEM((NTP, 24, HD), F32),
    att=pltpu.VMEM((2, 8, HD), F32),
    sems=pltpu.SemaphoreType.DMA((N_SEMS,)),
)
INPUTS = ("tok_in", "wg_in", "wu_in", "hgrad_in", "kv_in", "q_in", "nkv_in", "table", "lens", "owners")
OUTPUTS = ("ig_out", "gg_out", "gu_out", "at_out")


class Refs:
    def __init__(self, names, refs):
        for name, ref in zip(names, refs):
            setattr(self, name, ref)


def kernel(*refs):
    m = Refs(INPUTS + OUTPUTS + tuple(SCRATCH), refs)
    rep = lax.axis_index("rep")
    tp = lax.axis_index("tp")
    tail = lax.axis_index("tail")
    x, ylo = rep // 2, rep % 2
    z, core = tp // 2, tp % 2
    other = 1 - tail
    quarter, far_quarter = core * 2 + tail, core * 2 + other

    sib = {"tp": z * 2 + (1 - core)}
    yhi = {"tail": other}
    ypair = {"rep": x * 2 + (1 - ylo)}

    def zdev(d):
        return {"tp": lax.rem(z + d + NZ, NZ) * 2 + core}

    def xdev(d):
        return {"rep": lax.rem(x + d + NX, NX) * 2 + ylo}

    used = [0]

    def sem(count=1):
        first = used[0]
        used[0] += count
        return m.sems.at[first] if count == 1 else first

    outgoing = []

    def remote(src, dst, recv, dev):
        copy = pltpu.make_async_remote_copy(
            src_ref=src, dst_ref=dst, send_sem=sem(), recv_sem=recv, device_id=dev, device_id_type=MESH
        )
        copy.start()
        outgoing.append(copy)

    def arrived(dst, recv):
        pltpu.make_async_remote_copy(
            src_ref=dst, dst_ref=dst, send_sem=recv, recv_sem=recv, device_id=sib, device_id_type=MESH
        ).wait_recv()

    def plane_at(o):
        return lax.rem(z + o + NZ, NZ)

    tok_copy = pltpu.make_async_copy(m.tok_in, m.tok, sem())
    tok_copy.start()
    kv_copy = pltpu.make_async_copy(m.kv_in, m.kv, sem())
    kv_copy.start()
    w_sem = sem(2 * NZ)
    load_order = (0, -1, 1, -2, 2, -3, 3, 4)

    def weight_copies(o):
        plane, slot = plane_at(o), 2 * (o % NZ)
        return (
            pltpu.make_async_copy(m.wg_in.at[plane], m.wg.at[plane], m.sems.at[w_sem + slot]),
            pltpu.make_async_copy(m.wu_in.at[plane], m.wu.at[plane], m.sems.at[w_sem + slot + 1]),
        )

    for o in load_order:
        for copy in weight_copies(o):
            copy.start()
    hgrad_copy = pltpu.make_async_copy(m.hgrad_in, m.hgrad, sem())
    hgrad_copy.start()

    barrier = pltpu.get_barrier_semaphore()
    for d in range(1, NTP):
        pl.semaphore_signal(barrier, inc=1, device_id={"tp": lax.rem(tp + d, NTP)}, device_id_type=MESH)
    for d in range(1, NR):
        pl.semaphore_signal(barrier, inc=1, device_id={"rep": lax.rem(rep + d, NR)}, device_id_type=MESH)
    pl.semaphore_signal(barrier, inc=1, device_id=yhi, device_id_type=MESH)
    swap = {"rep": z, "tp": rep * 2 + core}

    @pl.when(z != rep)
    def _():
        pl.semaphore_signal(barrier, inc=1, device_id=swap, device_id_type=MESH)

    tok_copy.wait()
    m.xt[z, quarter] = m.tok[...].T
    pl.semaphore_wait(barrier, NTP - 1 + NR - 1 + 1 + jnp.where(z == rep, 0, 1))

    last_hop = {(1, 0): 4, (1, 1): 3, (-1, 0): 3, (-1, 1): 4}

    class Ring:
        def __init__(self, buf):
            self.buf = buf
            self.recv = [[sem() for _ in range(2)] for _ in range(NZ)]
            self.from_sib = [[sem() for _ in range(2)] for _ in range(NZ)]

        def block(self, o, s):
            return self.buf.at[plane_at(o), quarter if s == 0 else far_quarter]

        def sib_block(self, o, s):
            return self.buf.at[plane_at(o), (1 - core) * 2 + (tail if s == 0 else other)]

        def to_sib(self, o, s):
            remote(self.block(o, s), self.block(o, s), self.from_sib[o % NZ][s], sib)

        def along(self, o, s, d):
            remote(self.block(o, s), self.block(o, s), self.recv[(o - d) % NZ][s], zdev(d))

        def exchange(self):
            remote(self.block(0, 0), self.block(0, 0), self.recv[0][1], yhi)

        def start(self, s):
            if s == 1:
                arrived(self.block(0, 1), self.recv[0][1])
            for d in (1, -1):
                self.along(0, s, d)
            self.to_sib(0, s)

        def hop(self, h):
            for s in (0, 1):
                for d in (1, -1):
                    if h <= last_hop[d, s]:
                        o = -d * h
                        arrived(self.block(o, s), self.recv[o % NZ][s])
                        if h < last_hop[d, s]:
                            self.along(o, s, d)
                        self.to_sib(o, s)

        def rest(self, o):
            for s in (0, 1):
                arrived(self.sib_block(o, s), self.from_sib[o % NZ][s])

    ring = Ring(m.xt)
    ring2 = Ring(m.yt)
    swap_sem, swap_send = sem(), sem()

    ring.exchange()
    ring.start(0)
    swapped = pltpu.make_async_remote_copy(
        src_ref=m.xt.at[z, quarter],
        dst_ref=m.yt.at[rep, quarter],
        send_sem=swap_send,
        recv_sem=swap_sem,
        device_id=swap,
        device_id_type=MESH,
    )

    @pl.when(z != rep)
    def _():
        swapped.start()

    @pl.when(z == rep)
    def _():
        m.yt[z, quarter] = m.xt[z, quarter]

    m.kf[...] = jnp.zeros_like(m.kf)
    for n in range(2):
        m.kf[n * 2 : n * 2 + 2, :] = m.nkv_in[n].astype(F32)
        for head in range(32):
            g, q = head // 8, head % 8
            m.qs[g, q * 4 + n * 2 : q * 4 + n * 2 + 2, :] = m.q_in[n, :, head * HD : (head + 1) * HD].astype(F32)
    lane = lax.broadcasted_iota(jnp.int32, (8, POS), 1)
    row_tail = lax.broadcasted_iota(jnp.int32, (8, POS), 0) // 2 % 2
    page, offset = lane // 16, lane % 16
    places = []
    for n in range(2):
        place = jnp.full((8, POS), 1 << 20, jnp.int32)
        for b in range(16):
            place = jnp.where(page == m.table[n, b], tp * CPD + b * 16 + offset, place)
        places.append(place)
    home = rep * 2 + tail
    limit = jnp.where(row_tail == 0, m.lens[home * 2], m.lens[home * 2 + 1])
    live = (jnp.where(row_tail == 0, places[0], places[1]) < limit).astype(jnp.int32)
    live = jnp.concatenate([live] * 4, axis=0) > 0
    f_row = lax.broadcasted_iota(jnp.int32, (32, 16), 0)
    f_col = lax.broadcasted_iota(jnp.int32, (32, 16), 1)
    f_live = (f_col // 2 == f_row // 2 % 2) & (f_col % 2 <= f_row % 2) & (f_col + 16 * tp < 4)
    kv_copy.wait()
    for g in range(KVH):
        cols, vcols = slice(g * HD, (g + 1) * HD), slice((KVH + g) * HD, (KVH + g + 1) * HD)
        q = m.qs[g].astype(BF16)
        s = lax.dot_general(q, m.kv[:, cols], NT, preferred_element_type=F32) * HD ** (-0.5)
        fs = lax.dot_general(q, m.kf[:, cols].astype(BF16), NT, preferred_element_type=F32) * HD ** (-0.5)
        s, fs = jnp.where(live, s, MASK_VALUE), jnp.where(f_live, fs, MASK_VALUE)
        top = jnp.maximum(jnp.max(s, axis=1, keepdims=True), jnp.max(fs, axis=1, keepdims=True))
        p = jnp.where(live, jnp.exp(s - top), 0.0)
        fp = jnp.where(f_live, jnp.exp(fs - top), 0.0)
        total = jnp.sum(p, axis=1, keepdims=True) + jnp.sum(fp, axis=1, keepdims=True)
        out = jnp.dot(p.astype(BF16), m.kv[:, vcols], preferred_element_type=F32) + jnp.dot(
            fp.astype(BF16), m.kf[:, vcols].astype(BF16), preferred_element_type=F32
        )
        for j in range(4):
            rows = slice(j * 8, j * 8 + 8)
            m.ao[g * 4 + j, 0:8] = out[rows]
            m.ao[g * 4 + j, 8:16] = jnp.broadcast_to(top[rows], (8, HD))
            m.ao[g * 4 + j, 16:24] = jnp.broadcast_to(total[rows], (8, HD))

    ring.start(1)
    ar_sems = [None] + [sem() for _ in range(1, NTP)]
    for d in range(1, NTP):
        to = lax.rem(tp + d, NTP)
        remote(m.ao.at[to], m.ar.at[tp], ar_sems[d], {"tp": to})
    m.ar[tp] = m.ao[tp]

    m.hg[...] = jnp.zeros_like(m.hg)
    m.hu[...] = jnp.zeros_like(m.hu)

    def project(o):
        for copy in weight_copies(o):
            copy.wait()
        ring.rest(o)
        plane = plane_at(o)
        block = m.xt[plane].reshape(4 * ROWS, TOK).T
        m.hg[...] += jnp.dot(block, m.wg[plane].reshape(4 * ROWS, HID), preferred_element_type=F32)
        m.hu[...] += jnp.dot(block, m.wu[plane].reshape(4 * ROWS, HID), preferred_element_type=F32)

    ring.hop(1)
    project(0)
    ring.hop(2)

    @pl.when(z != rep)
    def _():
        swapped.wait_recv()

    ring2.exchange()
    project(-1)
    project(1)
    ring.hop(3)
    ring2.start(0)
    project(-2)
    project(2)
    ring.hop(4)
    ring2.start(1)
    project(-3)
    project(3)
    project(4)

    hgrad_copy.wait()
    gate = m.hg[...]
    sg = jax.nn.sigmoid(gate)
    grad_out = m.hgrad[...].astype(F32)
    m.ag[rep] = (grad_out * m.hu[...] * sg * (1.0 + gate * (1.0 - sg))).T.astype(BF16)
    m.au[rep] = (grad_out * gate * sg).T.astype(BF16)

    def slot(o, pair=False):
        return lax.rem(x + o + NX, NX) * 2 + ((1 - ylo) if pair else ylo)

    halves = {1: pl.ds(0, LO), -1: pl.ds(LO, HID - LO)}
    whole = pl.ds(0, HID)

    def push(buf, s, part, recv, dev):
        ref = buf.at[s, part]
        remote(ref, ref, recv, dev)

    g_pair = sem()
    g_near = {(s, d): sem() for s in (0, 1) for d in (1, -1)}
    g_far = {(s, d): sem() for s in (0, 1) for d in (1, -1)}
    u_near = {d: sem() for d in (1, -1)}
    u_far = {d: sem() for d in (1, -1)}
    u_pair = {key: sem() for key in ("own", "up", "down", 1, -1)}

    push(m.ag, rep, whole, g_pair, ypair)
    for d in (1, -1):
        push(m.au, rep, whole, u_near[d], xdev(d))
    push(m.au, rep, whole, u_pair["own"], ypair)
    for d in (1, -1):
        push(m.ag, rep, whole, g_near[0, d], xdev(d))

    sb_sems = [sem() for _ in range(NZ)]

    def partial(o):
        plane = plane_at(o)
        for half in (1 - core, core):
            value = jnp.dot(m.wg[plane, half], m.ag[rep], preferred_element_type=F32) + jnp.dot(
                m.wu[plane, half], m.au[rep], preferred_element_type=F32
            )
            if half is core:
                m.pf[plane] = value.reshape(2, ROWS, TOK)
            else:
                m.ss[plane] = value.reshape(2, ROWS, TOK).astype(BF16)
                remote(m.ss.at[plane], m.sb.at[plane], sb_sems[o % NZ], sib)

    chain = {(-1, 0): 4, (-1, 1): 3, (1, 0): 3, (1, 1): 4}
    places_of, count = {}, 0
    for key, length in chain.items():
        for i in range(1, length + 1):
            places_of[key + (i,)] = count
            count += 1
    rb_sems = [sem() for _ in range(count)]

    def own_term(o, c):
        plane = plane_at(o)
        return m.pf[plane, c] + m.sb[plane, c].astype(F32)

    def taken(d, c, i):
        place = places_of[d, c, i]
        arrived(m.rb.at[place], rb_sems[place])
        return m.rb[place].astype(F32)

    ready = set()

    def need(o):
        if o % NZ not in ready:
            ready.add(o % NZ)
            arrived(m.sb.at[plane_at(o)], sb_sems[o % NZ])

    def reduce_step(i):
        for d, c in ((-1, 0), (1, 1), (-1, 1), (1, 0)):
            if i <= chain[d, c]:
                o = d * (chain[d, c] - i + 1)
                need(o)
                value = own_term(o, c)
                if i > 1:
                    value += taken(d, c, i - 1)
                place = places_of[d, c, i]
                m.rs[place] = value.astype(BF16)
                remote(m.rs.at[place], m.rb.at[place], rb_sems[place], zdev(d))

    m.dg[...] = jnp.zeros_like(m.dg)
    m.du[...] = jnp.zeros_like(m.du)

    def weight_grad(total, act, s):
        def part(i, carry):
            rows = m.yt[s, pl.ds(i * 2, 2)].reshape(2 * ROWS, TOK)
            total[i] += lax.dot_general(rows, act[s], NT, preferred_element_type=F32)
            return carry

        lax.fori_loop(0, 2, part, 0)

    partial(4)
    partial(-3)
    partial(3)
    ring2.hop(1)
    arrived(m.ag.at[slot(0, True)], g_pair)
    for d in (1, -1):
        push(m.ag, slot(0, True), whole, g_near[1, d], xdev(d))
    partial(-2)
    partial(2)
    reduce_step(1)
    partial(-1)
    partial(1)
    ring2.hop(2)
    partial(0)
    for d in (1, -1):
        arrived(m.au.at[slot(-d)], u_near[d])
        push(m.au, slot(-d), halves[d], u_far[d], xdev(d))
        push(m.au, slot(-d), whole, u_pair["up" if d == 1 else "down"], ypair)
    reduce_step(2)
    ring2.hop(3)

    for d in range(1, NTP):
        arrived(m.ar.at[lax.rem(tp - d + NTP, NTP)], ar_sems[d])
    tops = m.ar[:, 8:16]
    weights = jnp.exp(tops - jnp.max(tops, axis=0, keepdims=True))
    m.att[tail] = jnp.sum(weights * m.ar[:, 0:8], axis=0) / jnp.sum(weights * m.ar[:, 16:24], axis=0)
    att_sem = sem()
    remote(m.att.at[tail], m.att.at[tail], att_sem, yhi)

    for d in (1, -1):
        arrived(m.ag.at[slot(-d)], g_near[0, d])
        push(m.ag, slot(-d), halves[d], g_far[0, d], xdev(d))
    reduce_step(3)
    ring2.hop(4)
    for d in (1, -1):
        arrived(m.ag.at[slot(-d, True)], g_near[1, d])
        push(m.ag, slot(-d, True), halves[d], g_far[1, d], xdev(d))
    reduce_step(4)
    for o in load_order:
        ring2.rest(o)
    weight_grad(m.dg, m.ag, rep)
    weight_grad(m.du, m.au, rep)
    for d in (1, -1):
        arrived(m.au.at[slot(2), halves[d]], u_far[d])
        push(m.au, slot(2), halves[d], u_pair[d], ypair)
    weight_grad(m.dg, m.ag, slot(0, True))
    for d in (1, -1):
        weight_grad(m.du, m.au, slot(-d))
        weight_grad(m.dg, m.ag, slot(-d))

    need(0)
    for c in (0, 1):
        m.fin[c] = own_term(0, c) + taken(-1, c, chain[-1, c]) + taken(1, c, chain[1, c])
    m.ysend[...] = m.fin[other].astype(BF16)
    y_sem = sem()
    remote(m.ysend, m.yrecv, y_sem, yhi)

    weight_grad(m.du, m.au, slot(2))
    for d in (1, -1):
        weight_grad(m.dg, m.ag, slot(-d, True))

    arrived(m.att.at[other], att_sem)
    for s in range(2):
        first = m.owners[(rep * 2 + s) * 2, 0]
        second = m.owners[(rep * 2 + s) * 2 + 1, 0]
        for step in range(2):
            for hp in range(2):
                cols = slice(hp * HD, (hp + 1) * HD)
                a = m.att[s, hp * 4 + step : hp * 4 + step + 1]
                b = m.att[s, hp * 4 + 2 + step : hp * 4 + 2 + step + 1]
                none = jnp.zeros_like(a)
                row = s * 4 + step
                m.at_out[row : row + 1, cols] = jnp.where(first == tail, a, jnp.where(second == tail, b, none))
                m.at_out[row + 2 : row + 3, cols] = jnp.where(
                    first == tail, jnp.where(second == tail, b, none), none
                )

    arrived(m.yrecv, y_sem)
    m.ig_out[...] = (m.fin[tail] + m.yrecv[...].astype(F32)).T.astype(BF16)

    arrived(m.au.at[slot(0, True)], u_pair["own"])
    weight_grad(m.du, m.au, slot(0, True))
    for d in (1, -1):
        arrived(m.au.at[slot(-d, True)], u_pair["up" if d == 1 else "down"])
        weight_grad(m.du, m.au, slot(-d, True))
    for s in (0, 1):
        for d in (1, -1):
            arrived(m.ag.at[slot(2, s == 1), halves[d]], g_far[s, d])
        weight_grad(m.dg, m.ag, slot(2, s == 1))
    for d in (1, -1):
        arrived(m.au.at[slot(2, True), halves[d]], u_pair[d])
    weight_grad(m.du, m.au, slot(2, True))
    for i in range(2):
        m.gg_out[i] = (m.dg[i] * SCALE).astype(BF16)
        m.gu_out[i] = (m.du[i] * SCALE).astype(BF16)

    for copy in outgoing:
        copy.wait_send()

    @pl.when(z != rep)
    def _():
        swapped.wait_send()

    assert used[0] <= N_SEMS, used[0]


def per_device(
    tokens, w_gate, w_up, hidden_grad, kv_pool, block_table, tail_len, tail_owner, new_queries, new_kv
):
    hbm = pl.BlockSpec(memory_space=pl.ANY)
    vmem = pl.BlockSpec(memory_space=pltpu.VMEM)
    smem = pl.BlockSpec(memory_space=pltpu.SMEM)
    input_grad, grad_gate, grad_up, attn = pl.pallas_call(
        kernel,
        out_shape=(
            jax.ShapeDtypeStruct((TOK, ROWS), BF16),
            jax.ShapeDtypeStruct((2, 2 * ROWS, HID), BF16),
            jax.ShapeDtypeStruct((2, 2 * ROWS, HID), BF16),
            jax.ShapeDtypeStruct((8, 2 * HD), F32),
        ),
        in_specs=[hbm] * 5 + [vmem] * 2 + [smem] * 3,
        out_specs=(vmem,) * 4,
        scratch_shapes=list(SCRATCH.values()),
        compiler_params=pltpu.CompilerParams(
            collective_id=0, has_side_effects=True, vmem_limit_bytes=60 * 2**20
        ),
        cost_estimate=pl.CostEstimate(flops=6_300_000_000, bytes_accessed=12_000_000, transcendentals=300_000),
    )(
        tokens,
        w_gate.reshape(NZ, 2, 2 * ROWS, HID),
        w_up.reshape(NZ, 2, 2 * ROWS, HID),
        hidden_grad,
        kv_pool.reshape(POS, 1024),
        new_queries,
        new_kv,
        block_table,
        tail_len,
        tail_owner,
    )
    return (
        input_grad,
        grad_gate.reshape(4 * ROWS, HID),
        grad_up.reshape(4 * ROWS, HID),
        attn.astype(BF16).reshape(4, 2, 2 * HD),
    )


def solution(mesh):
    in_specs = (
        P("rep", ("tp", "tail")),
        P(None, ("tp", "tail")),
        P(None, ("tp", "tail")),
        P("rep", ("tp", "tail")),
        P(("rep", "tp", "tail"), None, None),
        P(("rep", "tail"), "tp"),
        P(),
        P(),
        P(("rep", "tail"), None, None),
        P(("rep", "tail"), None, None),
    )
    out_specs = (
        P("rep", ("tp", "tail")),
        P("rep", ("tp", "tail")),
        P("rep", ("tp", "tail")),
        P(("rep", "tail"), None, "tp"),
    )
    return jax.shard_map(
        per_device, mesh=mesh, in_specs=in_specs, out_specs=out_specs, check_vma=False
    )
```

```python
import functools

import jax
import jax.numpy as jnp
from jax import lax
from jax.experimental import pallas as pl
from jax.experimental.pallas import tpu as pltpu
from jax.sharding import PartitionSpec as P

NR = 8
NZ = 8
NX = 4
ROWS = 160
TOK = 256
PLANE = 4 * ROWS
HALF = TOK // 2
PART = TOK // 4
HID = 400
ACTS = 2 * HID
CUT = 448
KVH = 4
HD = 128
CPD = 256
POS = 512
MASK_VALUE = -1e30
SCALE = 2048 ** (-0.5)
F32 = jnp.float32
BF16 = jnp.bfloat16
NT = (((1,), (1,)), ((), ()))
MESH = pl.DeviceIdType.MESH
SENDS = 24
N_SEMS = 178

SCRATCH = dict(
    xt=pltpu.VMEM((NZ, 4, 2, ROWS // 2, TOK), BF16),
    yt=pltpu.VMEM((NR, 4, 2, ROWS // 2, TOK), BF16),
    w=pltpu.VMEM((NZ, ACTS, PLANE), BF16),
    hgrad=pltpu.VMEM((HID, TOK), BF16),
    h=pltpu.VMEM((ACTS, TOK), F32),
    act=pltpu.VMEM((NR, ACTS, TOK), BF16),
    tact=pltpu.VMEM((2, TOK, HID), BF16),
    pf=pltpu.VMEM((NZ, 2, 2, PART, PLANE), F32),
    ss=pltpu.VMEM((NZ, 2, PART, PLANE), BF16),
    sb=pltpu.VMEM((NZ, 2, PART, PLANE), BF16),
    rs=pltpu.VMEM((14, PART, PLANE), BF16),
    rb=pltpu.VMEM((14, PART, PLANE), BF16),
    fin=pltpu.VMEM((4, ROWS, HALF), F32),
    fsend=pltpu.VMEM((2, ROWS, HALF), BF16),
    fsib=pltpu.VMEM((ROWS, HALF), F32),
    frecv=pltpu.VMEM((2, ROWS, HALF), BF16),
    dw=pltpu.VMEM((ACTS, PLANE), F32),
    kv=pltpu.VMEM((POS, 1024), BF16),
    q=pltpu.VMEM((2, 2, 4096), BF16),
    nkv=pltpu.VMEM((2, 2, 1024), BF16),
    qs=pltpu.VMEM((KVH, 32, HD), F32),
    kf=pltpu.VMEM((16, 1024), F32),
    ao=pltpu.VMEM((2, NZ, 16, HD), F32),
    asib=pltpu.VMEM((NZ, 16, HD), F32),
    am=pltpu.VMEM((NZ, 16, HD), F32),
    ar=pltpu.VMEM((NZ, 16, HD), F32),
    att=pltpu.VMEM((2, 8, HD), F32),
    ig=pltpu.VMEM((ROWS, TOK), BF16),
    og=pltpu.VMEM((ACTS, PLANE), BF16),
    at=pltpu.VMEM((4, 2, 2 * HD), BF16),
    table=pltpu.SMEM((2, 16), jnp.int32),
    lens=pltpu.SMEM((32,), jnp.int32),
    owners=pltpu.SMEM((32,), jnp.int32),
    sems=pltpu.SemaphoreType.DMA((N_SEMS,)),
)
INPUTS = ("tok_in", "wg_in", "wu_in", "hgrad_in", "kv_in", "q_in", "nkv_in", "table_in", "lens_in", "owners_in")
OUTPUTS = ("ig_out", "gg_out", "gu_out", "at_out")


class Refs:
    def __init__(self, names, refs):
        for name, ref in zip(names, refs):
            setattr(self, name, ref)


def kernel(*refs):
    m = Refs(INPUTS + OUTPUTS + tuple(SCRATCH), refs)
    rep = lax.axis_index("rep")
    tp = lax.axis_index("tp")
    tail = lax.axis_index("tail")
    x, ylo = rep // 2, rep % 2
    z, core = tp // 2, tp % 2
    other = 1 - tail
    quarter, far_quarter = core * 2 + tail, core * 2 + other

    sib = {"tp": z * 2 + (1 - core)}
    yhi = {"tail": other}
    diagonal = {"tp": z * 2 + (1 - core), "tail": other}
    ypair = {"rep": x * 2 + (1 - ylo)}

    def zdev(d):
        return {"tp": lax.rem(z + d + NZ, NZ) * 2 + core}

    def xdev(d):
        return {"rep": lax.rem(x + d + NX, NX) * 2 + ylo}

    def plane_at(o):
        return lax.rem(z + o + NZ, NZ)

    def slot(o, pair=False):
        return lax.rem(x + o + NX, NX) * 2 + ((1 - ylo) if pair else ylo)

    def far(f, back=False):
        dx = jnp.where(f < 2, 2, jnp.where((f == 2) != back, 1, 3))
        return lax.rem(x + dx, NX) * 2 + jnp.where(f == 0, ylo, 1 - ylo)

    used = [0]

    def sem(count=1):
        first = used[0]
        used[0] += count
        return m.sems.at[first] if count == 1 else first

    outgoing, outgoing_large = [], []
    first_send = sem(SENDS)

    def remote(src, dst, recv, dev, large=False):
        place = len(outgoing)
        if place >= SENDS and not large:
            outgoing[place - SENDS].wait_send()
        copy = pltpu.make_async_remote_copy(
            src_ref=src,
            dst_ref=dst,
            send_sem=sem() if large else m.sems.at[first_send + place % SENDS],
            recv_sem=recv,
            device_id=dev,
            device_id_type=MESH,
        )
        copy.start()
        (outgoing_large if large else outgoing).append(copy)

    def arrived(dst, recv):
        pltpu.make_async_remote_copy(
            src_ref=dst, dst_ref=dst, send_sem=recv, recv_sem=recv, device_id=sib, device_id_type=MESH
        ).wait_recv()

    barrier = pltpu.get_barrier_semaphore()

    def greet(dev):
        pl.semaphore_signal(barrier, inc=1, device_id=dev, device_id_type=MESH)

    peers = [zdev(d) for d in range(1, NZ)] + [{"rep": lax.rem(rep + d, NR)} for d in range(1, NR)]
    peers += [sib, yhi, diagonal]
    for dev in peers:
        greet(dev)

    def load(src, dst, on=None):
        copy = pltpu.make_async_copy(src, dst, sem() if on is None else on)
        copy.start()
        return copy

    small_sems = [sem() for _ in range(6)]
    small_loads = [
        load(m.table_in, m.table, small_sems[0]),
        load(m.lens_in, m.lens, small_sems[1]),
        load(m.owners_in, m.owners, small_sems[2]),
        load(m.q_in, m.q, small_sems[3]),
        load(m.nkv_in, m.nkv, small_sems[4]),
        load(m.kv_in, m.kv, small_sems[5]),
    ]
    tok_load = load(m.tok_in, m.xt.at[z, quarter])
    w_loads = {}
    for o in (0, -1, 1, -2, 2, -3, 3, 4):
        plane = plane_at(o)
        cols = pl.ds(pl.multiple_of(plane * PLANE, 128), PLANE)
        w_sem = sem()
        load(m.wg_in.at[:, cols], m.w.at[plane, pl.ds(0, HID)], w_sem)
        load(m.wu_in.at[:, cols], m.w.at[plane, pl.ds(HID, HID)], w_sem)
        w_loads[o] = pltpu.make_async_copy(m.w.at[plane], m.w.at[plane], w_sem)
    hgrad_load = load(m.hgrad_in, m.hgrad)

    for copy in small_loads:
        copy.wait()
    m.kf[...] = jnp.zeros_like(m.kf)
    for n in range(2):
        m.kf[n * 2 : n * 2 + 2, :] = m.nkv[n].astype(F32)
        for head in range(32):
            g, q = head // 8, head % 8
            m.qs[g, q * 4 + n * 2 : q * 4 + n * 2 + 2, :] = m.q[n, :, head * HD : (head + 1) * HD].astype(F32)
    lane = lax.broadcasted_iota(jnp.int32, (8, POS), 1)
    row_tail = lax.broadcasted_iota(jnp.int32, (8, POS), 0) // 2 % 2
    page, offset = lane // 16, lane % 16
    places = []
    for n in range(2):
        place = jnp.full((8, POS), 1 << 20, jnp.int32)
        for b in range(16):
            place = jnp.where(page == m.table[n, b], tp * CPD + b * 16 + offset, place)
        places.append(place)
    home = rep * 2 + tail
    limit = jnp.where(row_tail == 0, m.lens[home * 2], m.lens[home * 2 + 1])
    live = (jnp.where(row_tail == 0, places[0], places[1]) < limit).astype(jnp.int32)
    live = jnp.concatenate([live] * 4, axis=0) > 0
    f_row = lax.broadcasted_iota(jnp.int32, (32, 16), 0)
    f_col = lax.broadcasted_iota(jnp.int32, (32, 16), 1)
    f_live = (f_col // 2 == f_row // 2 % 2) & (f_col % 2 <= f_row % 2) & (f_col + 16 * tp < 4)
    low_lanes = lax.broadcasted_iota(jnp.int32, (8, HD), 1) < HD // 2

    def both(top, total):
        return jnp.where(low_lanes, top, total)

    for g in range(KVH):
        cols, vcols = slice(g * HD, (g + 1) * HD), slice((KVH + g) * HD, (KVH + g + 1) * HD)
        q = m.qs[g].astype(BF16)
        s = lax.dot_general(q, m.kv[:, cols], NT, preferred_element_type=F32) * HD ** (-0.5)
        fs = lax.dot_general(q, m.kf[:, cols].astype(BF16), NT, preferred_element_type=F32) * HD ** (-0.5)
        s, fs = jnp.where(live, s, MASK_VALUE), jnp.where(f_live, fs, MASK_VALUE)
        top = jnp.maximum(jnp.max(s, axis=1, keepdims=True), jnp.max(fs, axis=1, keepdims=True))
        p = jnp.where(live, jnp.exp(s - top), 0.0)
        fp = jnp.where(f_live, jnp.exp(fs - top), 0.0)
        total = jnp.sum(p, axis=1, keepdims=True) + jnp.sum(fp, axis=1, keepdims=True)
        out = jnp.dot(p.astype(BF16), m.kv[:, vcols], preferred_element_type=F32) + jnp.dot(
            fp.astype(BF16), m.kf[:, vcols].astype(BF16), preferred_element_type=F32
        )
        for j in range(4):
            rows = slice(j * 8, j * 8 + 8)
            to = g * 4 + j
            m.ao[to % 2, to // 2, 0:8] = out[rows]
            m.ao[to % 2, to // 2, 8:16] = both(top[rows], total[rows])

    tok_load.wait()
    pl.semaphore_wait(barrier, len(peers))

    class Ring:
        def __init__(self, place, pieces, across):
            self.place = place
            self.pieces = range(pieces)
            self.across = across
            self.last_hop = {(1, 0): 4, (1, 1): 3, (-1, 0): 3, (-1, 1): 3 if across else 4}
            self.recv = [[[sem() for _ in self.pieces] for _ in range(2)] for _ in range(NZ)]
            self.from_sib = [sem() for _ in range(NZ)]

        def piece(self, o, s, u=None):
            return self.place(plane_at(o), quarter if s == 0 else far_quarter, u)

        def to_sib(self, o, s):
            remote(self.piece(o, s), self.piece(o, s), self.from_sib[o % NZ], sib)

        def along(self, o, s, u, d):
            remote(self.piece(o, s, u), self.piece(o, s, u), self.recv[(o - d) % NZ][s][u], zdev(d))

        def exchange(self, o, u):
            remote(self.piece(o, 0, u), self.piece(o, 0, u), self.recv[o % NZ][1][u], yhi)

        def taken(self, o, s, u):
            arrived(self.piece(o, s, u), self.recv[o % NZ][s][u])

        def start(self, s):
            for u in self.pieces:
                if s == 1 and self.across:
                    self.taken(0, 1, u)
                for d in (1, -1):
                    self.along(0, s, u, d)
            self.to_sib(0, s)

        def hop(self, s, h):
            dirs = [d for d in (1, -1) if h <= self.last_hop[d, s]]
            for u in self.pieces:
                for d in dirs:
                    self.taken(-d * h, s, u)
                    if h < self.last_hop[d, s]:
                        self.along(-d * h, s, u, d)
                    if h == 4 and self.across:
                        self.exchange(4, u)
            for d in dirs:
                self.to_sib(-d * h, s)

        def last(self):
            for u in self.pieces:
                self.taken(4, 1, u)
            self.to_sib(4, 1)

        def rest(self, o):
            both = self.place(plane_at(o), pl.ds((1 - core) * 2, 2), None)
            arrived(both, self.from_sib[o % NZ])

    ring = Ring(lambda plane, q, u: m.xt.at[plane, q] if u is None else m.xt.at[plane, q, u], 2, True)
    ring2 = Ring(lambda plane, q, u: m.yt.at[far(plane // 2), q, plane % 2], 1, False)

    def project(o):
        w_loads[o].wait()
        ring.rest(o)
        plane = plane_at(o)
        for part in (pl.ds(0, HID), pl.ds(HID, HID)):
            value = jnp.dot(m.w[plane, part], m.xt[plane].reshape(PLANE, TOK), preferred_element_type=F32)
            if o == 0:
                m.h[part] = value
            else:
                m.h[part] += value

    def merged(parts):
        tops = [part[8:16, 0:1] for part in parts]
        top = functools.reduce(jnp.maximum, tops)
        scaling = [jnp.exp(t - top) for t in tops]
        out = sum(scale * part[0:8] for scale, part in zip(scaling, parts))
        total = sum(scale * part[8:16, HD // 2 : HD // 2 + 1] for scale, part in zip(scaling, parts))
        return out, top, total

    for u in (0, 1):
        ring.exchange(0, u)
        for d in (1, -1):
            ring.along(0, 0, u, d)
    ring.to_sib(0, 0)
    asib_sem = sem()
    remote(m.ao.at[1 - core], m.asib, asib_sem, sib)
    ring.hop(0, 1)
    ring.start(1)

    arrived(m.asib, asib_sem)
    for i in range(NZ):
        out, top, total = merged([m.ao[core, i], m.asib[i]])
        m.am[i, 0:8] = out
        m.am[i, 8:16] = both(top, total)

    ring.hop(0, 2)
    ring.hop(1, 1)
    project(0)
    ring.hop(0, 3)
    ring.hop(1, 2)
    ring.hop(0, 4)

    own_half, sib_half = pl.ds(core * 2, 2), pl.ds((1 - core) * 2, 2)
    near = {"pair": (slot(0, True), ypair), 1: (slot(1), xdev(1)), -1: (slot(-1), xdev(-1))}
    near_sems = {(key, s): sem() for key in near for s in (0, 1)}
    near_sib_sem = sem()
    first_sems = [sem(), sem()]
    target = far(z // 2, True)

    def seed(s):
        q = quarter if s == 0 else far_quarter
        remote(m.xt.at[target, q, z % 2], m.yt.at[rep, q, z % 2], first_sems[s], {"rep": target})

    def straight(s):
        q = quarter if s == 0 else far_quarter
        for key, (r, dev) in near.items():
            to = key if key == "pair" else -key
            remote(m.xt.at[r, q], m.yt.at[rep, q], near_sems[to, s], dev, True)

    seed(0)
    project(-1)
    project(1)
    ring.hop(1, 3)
    project(-2)
    project(2)
    ring.last()
    seed(1)
    straight(0)
    straight(1)
    ar_sem = sem()
    for d in range(1, NZ):
        remote(m.am.at[plane_at(d)], m.ar.at[z], ar_sem, zdev(d))
    m.ar[z] = m.am[z]
    project(-3)
    project(3)
    arrived(ring2.piece(0, 0), first_sems[0])
    ring2.start(0)
    project(4)

    hgrad_load.wait()
    gate, up = m.h[0:HID], m.h[HID:ACTS]
    sg = jax.nn.sigmoid(gate)
    grad_out = m.hgrad[...].astype(F32)
    act_gate = grad_out * up * sg * (1.0 + gate * (1.0 - sg))
    act_up = grad_out * gate * sg
    m.act[rep, 0:HID] = act_gate.astype(BF16)
    m.act[rep, HID:ACTS] = act_up.astype(BF16)

    first, second = pl.ds(0, CUT), pl.ds(CUT, ACTS - CUT)
    first_half = {1: pl.ds(0, CUT // 2), -1: pl.ds(CUT // 2, CUT // 2)}
    second_half = {1: pl.ds(CUT, (ACTS - CUT) // 2), -1: pl.ds((CUT + ACTS) // 2, (ACTS - CUT) // 2)}

    def push(s, part, recv, dev):
        ref = m.act.at[s, part]
        remote(ref, ref, recv, dev, True)

    g_pair = sem()
    g_near = {(s, d): sem() for s in (0, 1) for d in (1, -1)}
    g_far = {s: sem() for s in (0, 1)}
    u_near = {d: sem() for d in (1, -1)}
    u_far = sem()
    u_pair = {key: sem() for key in ("own", "up", "down", "far")}

    push(rep, first, g_pair, ypair)
    for d in (1, -1):
        push(rep, second, u_near[d], xdev(d))

    m.tact[0] = act_gate.T.astype(BF16)
    m.tact[1] = act_up.T.astype(BF16)

    sb_sems = [sem() for _ in range(NZ)]

    def partial(o):
        plane = plane_at(o)
        value = jnp.dot(m.tact[0], m.w[plane, pl.ds(0, HID)], preferred_element_type=F32) + jnp.dot(
            m.tact[1], m.w[plane, pl.ds(HID, HID)], preferred_element_type=F32
        )
        m.pf[plane] = value.reshape(2, 2, PART, PLANE)
        m.ss[plane] = m.pf[plane, 1 - core].astype(BF16)
        remote(m.ss.at[plane], m.sb.at[plane], sb_sems[o % NZ], sib)

    chain = {(-1, 0): 4, (-1, 1): 3, (1, 0): 3, (1, 1): 4}
    places_of, count = {}, 0
    for key, length in chain.items():
        for i in range(1, length + 1):
            places_of[key + (i,)] = count
            count += 1
    rb_sems = [sem() for _ in range(count)]

    def own_term(o, c):
        plane = plane_at(o)
        return m.pf[plane, core, c] + m.sb[plane, c].astype(F32)

    def taken(d, c, i):
        place = places_of[d, c, i]
        arrived(m.rb.at[place], rb_sems[place])
        return m.rb[place].astype(F32)

    ready = set()

    def need(o):
        if o % NZ not in ready:
            ready.add(o % NZ)
            arrived(m.sb.at[plane_at(o)], sb_sems[o % NZ])

    def reduce_step(i):
        for d, c in ((-1, 0), (1, 1), (-1, 1), (1, 0)):
            if i <= chain[d, c]:
                o = d * (chain[d, c] - i + 1)
                need(o)
                value = own_term(o, c)
                if i > 1:
                    value += taken(d, c, i - 1)
                place = places_of[d, c, i]
                m.rs[place] = value.astype(BF16)
                remote(m.rs.at[place], m.rb.at[place], rb_sems[place], zdev(d))

    def weight_grad(s, parts, tokens=None, fresh=False):
        rows = (m.yt if tokens is None else tokens)[s].reshape(PLANE, TOK)
        for part in parts:
            value = lax.dot_general(m.act[s, part], rows, NT, preferred_element_type=F32)
            if fresh:
                m.dw[part] = value
            else:
                m.dw[part] += value

    partial(4)
    arrived(ring2.piece(0, 1), first_sems[1])
    ring2.start(1)
    partial(-3)
    ring2.hop(0, 1)
    partial(3)
    reduce_step(1)
    for d in (1, -1):
        push(rep, first, g_near[0, d], xdev(d))
    push(rep, second, u_pair["own"], ypair)
    partial(-2)
    ring2.hop(1, 1)
    ring2.hop(0, 2)
    partial(2)
    for key, (r, _) in near.items():
        for s, q in ((0, quarter), (1, far_quarter)):
            arrived(m.yt.at[r, q], near_sems[key, s])
        remote(m.yt.at[r, own_half], m.yt.at[r, own_half], near_sib_sem, sib)
    partial(-1)
    for d in (1, -1):
        arrived(m.act.at[slot(-d), second], u_near[d])
        push(slot(-d), second, u_pair["up" if d == 1 else "down"], ypair)
        push(slot(-d), second_half[d], u_far, xdev(d))
    partial(1)
    arrived(m.act.at[slot(0, True), first], g_pair)
    for d in (1, -1):
        push(slot(0, True), first, g_near[1, d], xdev(d))
    partial(0)
    reduce_step(2)
    ring2.hop(1, 2)
    ring2.hop(0, 3)
    weight_grad(rep, (first, second), m.xt, True)
    for d in (1, -1):
        arrived(m.act.at[slot(-d), first], g_near[0, d])
        push(slot(-d), first_half[d], g_far[0], xdev(d))
    arrived(m.yt.at[pl.ds(0, 3), own_half], near_sib_sem)
    weight_grad(slot(1), (first, second))
    reduce_step(3)
    ring2.hop(1, 3)
    ring2.hop(0, 4)
    weight_grad(slot(-1), (first, second))
    weight_grad(slot(0, True), (first,))
    arrived(m.act.at[slot(2), second], u_far)
    push(slot(2), second, u_pair["far"], ypair)
    reduce_step(4)
    for d in (1, -1):
        arrived(m.act.at[slot(-d, True), first], g_near[1, d])
        push(slot(-d, True), first_half[d], g_far[1], xdev(d))

    arrived(m.ar.at[pl.ds(0, NZ - 1)], ar_sem)
    out, _, total = merged([m.ar[i] for i in range(NZ)])
    m.att[tail] = out / total
    att_sem = sem()
    remote(m.att.at[tail], m.att.at[tail], att_sem, yhi)

    ring2.hop(1, 4)
    for o in (0, -1, 1, -2, 2, -3, 3, 4):
        ring2.rest(o)

    need(0)
    value = jnp.concatenate(
        [own_term(0, c) + taken(-1, c, chain[-1, c]) + taken(1, c, chain[1, c]) for c in (0, 1)], axis=0
    )
    m.fin[...] = value.T.reshape(4, ROWS, HALF)
    m.fsend[0] = m.fin[far_quarter].astype(BF16)
    m.fsend[1] = m.fin[(1 - core) * 2 + other].astype(BF16)
    y_sem, diagonal_sem, fsib_sem = sem(), sem(), sem()
    remote(m.fsend.at[0], m.frecv.at[0], y_sem, yhi)
    remote(m.fsend.at[1], m.frecv.at[1], diagonal_sem, diagonal)
    remote(m.fin.at[(1 - core) * 2 + tail], m.fsib, fsib_sem, sib)

    weight_grad(slot(2), (second,))
    for d in (1, -1):
        weight_grad(slot(-d, True), (first,))

    arrived(m.act.at[slot(0, True), second], u_pair["own"])
    weight_grad(slot(0, True), (second,))
    for d in (1, -1):
        arrived(m.act.at[slot(-d, True), second], u_pair["up" if d == 1 else "down"])
        weight_grad(slot(-d, True), (second,))

    arrived(m.fsib, fsib_sem)
    arrived(m.frecv.at[0], y_sem)
    arrived(m.frecv.at[1], diagonal_sem)
    mine = pl.ds(pl.multiple_of(core * HALF, HALF), HALF)
    theirs = pl.ds(pl.multiple_of((1 - core) * HALF, HALF), HALF)
    m.ig[:, mine] = (m.fin[quarter] + m.frecv[0].astype(F32)).astype(BF16)
    m.ig[:, theirs] = (m.fsib[...] + m.frecv[1].astype(F32)).astype(BF16)
    stores = [load(m.ig, m.ig_out, small_sems[1])]

    arrived(m.att.at[other], att_sem)
    for s in range(2):
        owner0 = m.owners[(rep * 2 + s) * 2]
        owner1 = m.owners[(rep * 2 + s) * 2 + 1]
        for hp in range(2):
            cols = slice(hp * HD, (hp + 1) * HD)
            a = m.att[s, hp * 4 : hp * 4 + 2]
            b = m.att[s, hp * 4 + 2 : hp * 4 + 4]
            none = jnp.zeros_like(a)
            b = jnp.where(owner1 == tail, b, none)
            m.at[s * 2, :, cols] = jnp.where(owner0 == tail, a, b).astype(BF16)
            m.at[s * 2 + 1, :, cols] = jnp.where(owner0 == tail, b, none).astype(BF16)
    stores.append(load(m.at, m.at_out, small_sems[0]))

    for s in (0, 1):
        arrived(m.act.at[slot(2, s == 1), first], g_far[s])
        weight_grad(slot(2, s == 1), (first,))

    def store(i, out_ref):
        part = pl.ds(i * HID, HID)
        m.og[part] = (m.dw[part] * SCALE).astype(BF16)
        stores.append(load(m.og.at[part], out_ref, small_sems[2 + i]))

    store(0, m.gg_out)
    arrived(m.act.at[slot(2, True), second], u_pair["far"])
    weight_grad(slot(2, True), (second,))
    store(1, m.gu_out)

    for copy in outgoing[-SENDS:] + outgoing_large:
        copy.wait_send()
    for copy in stores:
        copy.wait()
    assert used[0] == N_SEMS, used[0]


def hand_on(*refs):
    for i in range(4):
        refs[4 + i][...] = refs[i][...]


def per_device(
    tokens, w_gate, w_up, hidden_grad, kv_pool, block_table, tail_len, tail_owner, new_queries, new_kv
):
    hbm = pl.BlockSpec(memory_space=pl.ANY)
    vmem = pl.BlockSpec(memory_space=pltpu.VMEM)
    out_shape = (
        jax.ShapeDtypeStruct((ROWS, TOK), BF16),
        jax.ShapeDtypeStruct((HID, PLANE), BF16),
        jax.ShapeDtypeStruct((HID, PLANE), BF16),
        jax.ShapeDtypeStruct((4, 2, 2 * HD), BF16),
    )
    results = pl.pallas_call(
        kernel,
        out_shape=out_shape,
        in_specs=[hbm] * 10,
        out_specs=(hbm,) * 4,
        scratch_shapes=list(SCRATCH.values()),
        compiler_params=pltpu.CompilerParams(
            collective_id=0, has_side_effects=True, vmem_limit_bytes=60 * 2**20
        ),
        cost_estimate=pl.CostEstimate(flops=6_300_000_000, bytes_accessed=12_000_000, transcendentals=300_000),
    )(
        tokens.T.reshape(2, ROWS // 2, TOK),
        w_gate.T,
        w_up.T,
        hidden_grad.T,
        kv_pool.reshape(POS, 1024),
        new_queries,
        new_kv,
        block_table,
        tail_len,
        tail_owner.reshape(-1),
    )
    input_grad, grad_gate, grad_up, attn = pl.pallas_call(
        hand_on,
        out_shape=out_shape,
        in_specs=[vmem] * 4,
        out_specs=(vmem,) * 4,
    )(*results)
    return input_grad.T, grad_gate.T, grad_up.T, attn


def solution(mesh):
    in_specs = (
        P("rep", ("tp", "tail")),
        P(None, ("tp", "tail")),
        P(None, ("tp", "tail")),
        P("rep", ("tp", "tail")),
        P(("rep", "tp", "tail"), None, None),
        P(("rep", "tail"), "tp"),
        P(),
        P(),
        P(("rep", "tail"), None, None),
        P(("rep", "tail"), None, None),
    )
    out_specs = (
        P("rep", ("tp", "tail")),
        P("rep", ("tp", "tail")),
        P("rep", ("tp", "tail")),
        P(("rep", "tail"), None, "tp"),
    )
    return jax.shard_map(
        per_device, mesh=mesh, in_specs=in_specs, out_specs=out_specs, check_vma=False
    )
```

```python
import functools

import jax
import jax.numpy as jnp
from jax import lax
from jax.experimental import pallas as pl
from jax.experimental.pallas import tpu as pltpu
from jax.sharding import PartitionSpec as P

NR = 8
NZ = 8
NX = 4
ROWS = 160
TOK = 256
PLANE = 4 * ROWS
HALF = TOK // 2
PART = TOK // 4
HID = 400
ACTS = 2 * HID
CUT = 448
KVH = 4
HD = 128
CPD = 256
POS = 512
MASK_VALUE = -1e30
SCALE = 2048 ** (-0.5)
F32 = jnp.float32
BF16 = jnp.bfloat16
NT = (((1,), (1,)), ((), ()))
MESH = pl.DeviceIdType.MESH
SENDS = 24
N_SEMS = 181

SCRATCH = dict(
    xt=pltpu.VMEM((NZ, 4, 2, ROWS // 2, TOK), BF16),
    yt=pltpu.VMEM((NR, 4, 2, ROWS // 2, TOK), BF16),
    w=pltpu.VMEM((NZ, ACTS, PLANE), BF16),
    hgrad=pltpu.VMEM((HID, TOK), BF16),
    h=pltpu.VMEM((ACTS, TOK), F32),
    act=pltpu.VMEM((NR, ACTS, TOK), BF16),
    tact=pltpu.VMEM((2, 2, HALF, HID), BF16),
    pf=pltpu.VMEM((NZ, 2, PART, PLANE), F32),
    ss=pltpu.VMEM((NZ, 2, PART, PLANE), BF16),
    sb=pltpu.VMEM((NZ, 2, PART, PLANE), BF16),
    rs=pltpu.VMEM((14, PART, PLANE), BF16),
    rb=pltpu.VMEM((14, PART, PLANE), BF16),
    fin=pltpu.VMEM((4, ROWS, HALF), F32),
    fsend=pltpu.VMEM((2, ROWS, HALF), BF16),
    fsib=pltpu.VMEM((ROWS, HALF), F32),
    frecv=pltpu.VMEM((2, ROWS, HALF), BF16),
    dw=pltpu.VMEM((ACTS, PLANE), F32),
    kv=pltpu.VMEM((POS, 1024), BF16),
    q=pltpu.VMEM((2, 2, 4096), BF16),
    nkv=pltpu.VMEM((2, 2, 1024), BF16),
    qs=pltpu.VMEM((KVH, 32, HD), F32),
    kf=pltpu.VMEM((16, 1024), F32),
    ao=pltpu.VMEM((2, NZ, 16, HD), F32),
    asib=pltpu.VMEM((NZ, 16, HD), F32),
    am=pltpu.VMEM((NZ, 16, HD), F32),
    asend=pltpu.VMEM((7, 16, HD), F32),
    ar=pltpu.VMEM((7, 16, HD), F32),
    att=pltpu.VMEM((2, 8, HD), F32),
    ig=pltpu.VMEM((ROWS, TOK), BF16),
    og=pltpu.VMEM((ACTS, PLANE), BF16),
    at=pltpu.VMEM((4, 2, 2 * HD), BF16),
    table=pltpu.SMEM((2, 16), jnp.int32),
    lens=pltpu.SMEM((32,), jnp.int32),
    owners=pltpu.SMEM((32,), jnp.int32),
    met=pltpu.SemaphoreType.REGULAR((2,)),
    sems=pltpu.SemaphoreType.DMA((N_SEMS,)),
)
INPUTS = ("tok_in", "wg_in", "wu_in", "hgrad_in", "kv_in", "q_in", "nkv_in", "table_in", "lens_in", "owners_in")
OUTPUTS = ("ig_out", "gg_out", "gu_out", "at_out")


class Refs:
    def __init__(self, names, refs):
        for name, ref in zip(names, refs):
            setattr(self, name, ref)


def kernel(*refs):
    m = Refs(INPUTS + OUTPUTS + tuple(SCRATCH), refs)
    rep = lax.axis_index("rep")
    tp = lax.axis_index("tp")
    tail = lax.axis_index("tail")
    x, ylo = rep // 2, rep % 2
    z, core = tp // 2, tp % 2
    other = 1 - tail
    quarter, far_quarter = core * 2 + tail, core * 2 + other

    sib = {"tp": z * 2 + (1 - core)}
    yhi = {"tail": other}
    diagonal = {"tp": z * 2 + (1 - core), "tail": other}
    ypair = {"rep": x * 2 + (1 - ylo)}

    def zdev(d):
        return {"tp": lax.rem(z + d + NZ, NZ) * 2 + core}

    def xdev(d):
        return {"rep": lax.rem(x + d + NX, NX) * 2 + ylo}

    def plane_at(o):
        return lax.rem(z + o + NZ, NZ)

    def slot(o, pair=False):
        return lax.rem(x + o + NX, NX) * 2 + ((1 - ylo) if pair else ylo)

    def far(f, back=False):
        dx = jnp.where(f < 2, 2, jnp.where((f == 2) != back, 1, 3))
        return lax.rem(x + dx, NX) * 2 + jnp.where(f == 0, ylo, 1 - ylo)

    used = [0]

    def sem(count=1):
        first = used[0]
        used[0] += count
        return m.sems.at[first] if count == 1 else first

    outgoing, outgoing_large = [], []
    first_send = sem(SENDS)

    def remote(src, dst, recv, dev, large=False):
        place = len(outgoing)
        if place >= SENDS and not large:
            outgoing[place - SENDS].wait_send()
        copy = pltpu.make_async_remote_copy(
            src_ref=src,
            dst_ref=dst,
            send_sem=sem() if large else m.sems.at[first_send + place % SENDS],
            recv_sem=recv,
            device_id=dev,
            device_id_type=MESH,
        )
        copy.start()
        (outgoing_large if large else outgoing).append(copy)

    def arrived(dst, recv):
        pltpu.make_async_remote_copy(
            src_ref=dst, dst_ref=dst, send_sem=recv, recv_sem=recv, device_id=sib, device_id_type=MESH
        ).wait_recv()

    barrier = pltpu.get_barrier_semaphore()

    def greet(dev, on=barrier):
        pl.semaphore_signal(on, inc=1, device_id=dev, device_id_type=MESH)

    target, source = far(z // 2, True), far(z // 2)
    peers = [zdev(1), zdev(-1), sib, yhi, ypair, xdev(1), xdev(-1)]
    for dev in peers:
        greet(dev)

    def load(src, dst, on=None):
        copy = pltpu.make_async_copy(src, dst, sem() if on is None else on)
        copy.start()
        return copy

    tok_load = load(m.tok_in, m.xt.at[z, quarter])
    class Ring:
        def __init__(self, place, pieces, across):
            self.place = place
            self.pieces = range(pieces)
            self.across = across
            near = 2 if across else 3
            self.last_hop = {(d, s, u): (3, near)[s] for d in (1, -1) for s in (0, 1) for u in self.pieces}
            self.last_hop[1, 0, 0] = 4
            self.last_hop[(-1, 0, 1) if across else (-1, 1, 0)] = 4
            self.recv = [[[sem() for _ in self.pieces] for _ in range(2)] for _ in range(NZ)]
            self.from_sib = [sem() for _ in range(NZ)]

        def piece(self, o, s, u=None):
            return self.place(plane_at(o), quarter if s == 0 else far_quarter, u)

        def to_sib(self, o, s):
            remote(self.piece(o, s), self.piece(o, s), self.from_sib[o % NZ], sib)

        def along(self, o, s, u, d):
            remote(self.piece(o, s, u), self.piece(o, s, u), self.recv[(o - d) % NZ][s][u], zdev(d))

        def exchange(self, o, u):
            remote(self.piece(o, 0, u), self.piece(o, 0, u), self.recv[o % NZ][1][u], yhi)

        def taken(self, o, s, u):
            arrived(self.piece(o, s, u), self.recv[o % NZ][s][u])

        def start(self, s):
            for u in self.pieces:
                if s == 1:
                    self.taken(0, 1, u)
                for d in (1, -1):
                    self.along(0, s, u, d)
            self.to_sib(0, s)

        def hop(self, s, h):
            whole = []
            for u in self.pieces:
                for d in (1, -1):
                    o = -d * h
                    if h <= self.last_hop[d, s, u]:
                        self.taken(o, s, u)
                        if h < self.last_hop[d, s, u]:
                            self.along(o, s, u, d)
                        if h >= 3 and s == 0 and self.across:
                            self.exchange(o, u)
                        if u == self.pieces[-1]:
                            whole.append(o)
            for o in whole:
                self.to_sib(o, s)

        def crossed(self, o):
            for u in self.pieces:
                self.taken(o, 1, u)
            self.to_sib(o, 1)

        def rest(self, o):
            both = self.place(plane_at(o), pl.ds((1 - core) * 2, 2), None)
            arrived(both, self.from_sib[o % NZ])

    ring = Ring(lambda plane, q, u: m.xt.at[plane, q] if u is None else m.xt.at[plane, q, u], 2, True)
    ring2 = Ring(lambda plane, q, u: m.yt.at[far(plane // 2), q, plane % 2], 1, False)

    tok_load.wait()
    pl.semaphore_wait(barrier, len(peers))

    for u in (0, 1):
        ring.exchange(0, u)
        for d in (1, -1):
            ring.along(0, 0, u, d)
    ring.to_sib(0, 0)

    small_sems = [sem() for _ in range(6)]
    small_loads = [
        load(m.table_in, m.table, small_sems[0]),
        load(m.lens_in, m.lens, small_sems[1]),
        load(m.owners_in, m.owners, small_sems[2]),
        load(m.q_in, m.q, small_sems[3]),
        load(m.nkv_in, m.nkv, small_sems[4]),
        load(m.kv_in, m.kv, small_sems[5]),
    ]
    w_loads = {}
    for o in (0, -1, 1, -2, 2, -3, 3, 4):
        plane = plane_at(o)
        cols = pl.ds(pl.multiple_of(plane * PLANE, 128), PLANE)
        w_sem = sem()
        load(m.wg_in.at[:, cols], m.w.at[plane, pl.ds(0, HID)], w_sem)
        load(m.wu_in.at[:, cols], m.w.at[plane, pl.ds(HID, HID)], w_sem)
        w_loads[o] = pltpu.make_async_copy(m.w.at[plane], m.w.at[plane], w_sem)
    hgrad_load = load(m.hgrad_in, m.hgrad)

    first_sem = sem()
    own_half = pl.ds(core * 2, 2)
    near = {"pair": (slot(0, True), ypair), 1: (slot(1), xdev(1)), -1: (slot(-1), xdev(-1))}
    near_sems = {key: sem() for key in near}
    near_sib_sem = sem()

    def later(src, dst, recv, dev):
        copy = pltpu.make_async_remote_copy(
            src_ref=src, dst_ref=dst, send_sem=sem(), recv_sem=recv, device_id=dev, device_id_type=MESH
        )
        outgoing_large.append(copy)
        return copy

    leaving = {0: [], 1: []}
    seed = later(m.xt.at[target, quarter, z % 2], m.yt.at[rep, quarter, z % 2], first_sem, {"rep": target})
    leaving[0].append((target, seed))
    for s, q in ((0, quarter), (1, far_quarter)):
        for key, (r, dev) in near.items():
            to = near_sems[key if key == "pair" else -key]
            leaving[s].append((r, later(m.xt.at[r, q], m.yt.at[rep, q], to, dev)))

    def leave(s, *hops):
        for r, copy in leaving[s]:
            away = lax.rem(r - z + NZ, NZ)
            now = functools.reduce(jnp.logical_or, [(away == h) | (away == NZ - h) for h in hops])
            pl.when(now)(copy.start)

    def project(o):
        w_loads[o].wait()
        ring.rest(o)
        plane = plane_at(o)
        for part in (pl.ds(0, HID), pl.ds(HID, HID)):
            value = jnp.dot(m.w[plane, part], m.xt[plane].reshape(PLANE, TOK), preferred_element_type=F32)
            if o == 0:
                m.h[part] = value
            else:
                m.h[part] += value

    def merged(parts):
        tops = [part[8:16, 0:1] for part in parts]
        top = functools.reduce(jnp.maximum, tops)
        scaling = [jnp.exp(t - top) for t in tops]
        out = sum(scale * part[0:8] for scale, part in zip(scaling, parts))
        total = sum(scale * part[8:16, HD // 2 : HD // 2 + 1] for scale, part in zip(scaling, parts))
        return out, top, total

    for copy in small_loads:
        copy.wait()
    m.kf[...] = jnp.zeros_like(m.kf)
    for n in range(2):
        m.kf[n * 2 : n * 2 + 2, :] = m.nkv[n].astype(F32)
        for head in range(32):
            g, q = head // 8, head % 8
            m.qs[g, q * 4 + n * 2 : q * 4 + n * 2 + 2, :] = m.q[n, :, head * HD : (head + 1) * HD].astype(F32)
    lane = lax.broadcasted_iota(jnp.int32, (8, POS), 1)
    row_tail = lax.broadcasted_iota(jnp.int32, (8, POS), 0) // 2 % 2
    page, offset = lane // 16, lane % 16
    places = []
    for n in range(2):
        place = jnp.full((8, POS), 1 << 20, jnp.int32)
        for b in range(16):
            place = jnp.where(page == m.table[n, b], tp * CPD + b * 16 + offset, place)
        places.append(place)
    home = rep * 2 + tail
    limit = jnp.where(row_tail == 0, m.lens[home * 2], m.lens[home * 2 + 1])
    live = (jnp.where(row_tail == 0, places[0], places[1]) < limit).astype(jnp.int32)
    live = jnp.concatenate([live] * 4, axis=0) > 0
    f_row = lax.broadcasted_iota(jnp.int32, (32, 16), 0)
    f_col = lax.broadcasted_iota(jnp.int32, (32, 16), 1)
    f_live = (f_col // 2 == f_row // 2 % 2) & (f_col % 2 <= f_row % 2) & (f_col + 16 * tp < 4)
    low_lanes = lax.broadcasted_iota(jnp.int32, (8, HD), 1) < HD // 2

    def both(top, total):
        return jnp.where(low_lanes, top, total)

    for g in range(KVH):
        cols, vcols = slice(g * HD, (g + 1) * HD), slice((KVH + g) * HD, (KVH + g + 1) * HD)
        q = m.qs[g].astype(BF16)
        s = lax.dot_general(q, m.kv[:, cols], NT, preferred_element_type=F32) * HD ** (-0.5)
        fs = lax.dot_general(q, m.kf[:, cols].astype(BF16), NT, preferred_element_type=F32) * HD ** (-0.5)
        s, fs = jnp.where(live, s, MASK_VALUE), jnp.where(f_live, fs, MASK_VALUE)
        top = jnp.maximum(jnp.max(s, axis=1, keepdims=True), jnp.max(fs, axis=1, keepdims=True))
        p = jnp.where(live, jnp.exp(s - top), 0.0)
        fp = jnp.where(f_live, jnp.exp(fs - top), 0.0)
        total = jnp.sum(p, axis=1, keepdims=True) + jnp.sum(fp, axis=1, keepdims=True)
        out = jnp.dot(p.astype(BF16), m.kv[:, vcols], preferred_element_type=F32) + jnp.dot(
            fp.astype(BF16), m.kf[:, vcols].astype(BF16), preferred_element_type=F32
        )
        for j in range(4):
            rows = slice(j * 8, j * 8 + 8)
            to = g * 4 + j
            m.ao[to % 2, to // 2, 0:8] = out[rows]
            m.ao[to % 2, to // 2, 8:16] = both(top[rows], total[rows])

    asib_sem = sem()
    remote(m.ao.at[1 - core], m.asib, asib_sem, sib)
    for dev in (sib, yhi, ypair, xdev(1), xdev(-1)):
        greet(dev, m.met.at[0])
    ring.hop(0, 1)
    ring.start(1)
    pl.semaphore_wait(m.met.at[0], 5)
    greet(ypair, m.met.at[1])
    ring.hop(0, 2)
    pl.semaphore_wait(m.met.at[1], 1)
    leave(0, 0, 1)
    ring.hop(1, 1)
    project(0)
    leave(1, 0)
    ring.hop(0, 3)
    leave(0, 2)
    ring.hop(1, 2)
    leave(1, 1)

    arrived(m.asib, asib_sem)
    for i in range(NZ):
        out, top, total = merged([m.ao[core, i], m.asib[i]])
        m.am[i, 0:8] = out
        m.am[i, 8:16] = both(top, total)

    ring.hop(0, 4)
    leave(0, 3, 4)
    project(-1)
    project(1)
    ring.crossed(-3)
    ring.crossed(3)
    leave(1, 2, 3)
    project(-2)
    project(2)
    arrived(ring2.piece(0, 0), first_sem)
    ring2.exchange(0, 0)
    ring2.start(0)
    ring.crossed(4)
    leave(1, 4)
    project(-3)
    project(3)
    project(4)

    hgrad_load.wait()
    gate, up = m.h[0:HID], m.h[HID:ACTS]
    sg = jax.nn.sigmoid(gate)
    grad_out = m.hgrad[...].astype(F32)
    act_gate = grad_out * up * sg * (1.0 + gate * (1.0 - sg))
    act_up = grad_out * gate * sg
    m.act[rep, 0:HID] = act_gate.astype(BF16)
    m.act[rep, HID:ACTS] = act_up.astype(BF16)

    first, second = pl.ds(0, CUT), pl.ds(CUT, ACTS - CUT)
    first_half = {1: pl.ds(0, CUT // 2), -1: pl.ds(CUT // 2, CUT // 2)}
    second_half = {1: pl.ds(CUT, (ACTS - CUT) // 2), -1: pl.ds((CUT + ACTS) // 2, (ACTS - CUT) // 2)}

    def push(s, part, recv, dev):
        ref = m.act.at[s, part]
        remote(ref, ref, recv, dev, True)

    g_pair = sem()
    g_near = {(s, d): sem() for s in (0, 1) for d in (1, -1)}
    g_far = {s: sem() for s in (0, 1)}
    u_near = {d: sem() for d in (1, -1)}
    u_far = sem()
    u_pair = {key: sem() for key in ("own", "up", "down", "far")}

    push(rep, first, g_pair, ypair)
    for d in (1, -1):
        push(rep, second, u_near[d], xdev(d))

    for i, value in enumerate((act_gate, act_up)):
        for half in (0, 1):
            m.tact[i, lax.rem(half + core, 2)] = value[:, half * HALF : (half + 1) * HALF].T.astype(BF16)


    sb_sems = [sem() for _ in range(NZ)]

    def partial(o):
        plane = plane_at(o)
        value = sum(
            jnp.dot(m.tact[i].reshape(TOK, HID), m.w[plane, pl.ds(i * HID, HID)], preferred_element_type=F32)
            for i in (0, 1)
        )
        m.pf[plane] = value[:HALF].reshape(2, PART, PLANE)
        m.ss[plane] = value[HALF:].reshape(2, PART, PLANE).astype(BF16)
        remote(m.ss.at[plane], m.sb.at[plane], sb_sems[o % NZ], sib)

    chain = {(-1, 0): 4, (-1, 1): 3, (1, 0): 3, (1, 1): 4}
    places_of, count = {}, 0
    for key, length in chain.items():
        for i in range(1, length + 1):
            places_of[key + (i,)] = count
            count += 1
    rb_sems = [sem() for _ in range(count)]

    def own_term(o, c):
        plane = plane_at(o)
        return m.pf[plane, c] + m.sb[plane, c].astype(F32)

    def taken(d, c, i):
        place = places_of[d, c, i]
        arrived(m.rb.at[place], rb_sems[place])
        return m.rb[place].astype(F32)

    ready = set()

    def need(o):
        if o % NZ not in ready:
            ready.add(o % NZ)
            arrived(m.sb.at[plane_at(o)], sb_sems[o % NZ])

    def reduce_step(i, longer):
        for d, c in ((-1, 0), (1, 1)) if longer else ((-1, 1), (1, 0)):
            o = d * (chain[d, c] - i + 1)
            need(o)
            value = own_term(o, c)
            if i > 1:
                value += taken(d, c, i - 1)
            place = places_of[d, c, i]
            m.rs[place] = value.astype(BF16)
            remote(m.rs.at[place], m.rb.at[place], rb_sems[place], zdev(d))

    ar_sems = [sem() for _ in range(7)]

    def earlier(d, i):
        place = i - 1 if d == -1 else 3 + i
        arrived(m.ar.at[place], ar_sems[place])
        return m.ar[place]

    def attention_step(i):
        for d, length in ((-1, 4), (1, 3)):
            if i <= length:
                place = i - 1 if d == -1 else 3 + i
                dest = plane_at(d * (length - i + 1))
                if i == 1:
                    m.asend[place] = m.am[dest]
                else:
                    out, top, total = merged([m.am[dest], earlier(d, i - 1)])
                    m.asend[place, 0:8] = out
                    m.asend[place, 8:16] = both(top, total)
                remote(m.asend.at[place], m.ar.at[place], ar_sems[place], zdev(d))

    def weight_grad(s, parts, tokens=None, fresh=False):
        rows = (m.yt if tokens is None else tokens)[s].reshape(PLANE, TOK)
        for part in parts:
            value = lax.dot_general(m.act[s, part], rows, NT, preferred_element_type=F32)
            if fresh:
                m.dw[part] = value
            else:
                m.dw[part] += value

    ring2.hop(0, 1)
    ring2.start(1)
    partial(4)
    partial(-3)
    partial(3)
    reduce_step(1, True)
    partial(-2)
    reduce_step(1, False)
    ring2.hop(0, 2)
    partial(2)
    for d in (1, -1):
        push(rep, first, g_near[0, d], xdev(d))
    partial(-1)
    partial(1)
    push(rep, second, u_pair["own"], ypair)
    ring2.hop(1, 1)
    attention_step(1)
    partial(0)
    for d in (1, -1):
        arrived(m.act.at[slot(-d), second], u_near[d])
        push(slot(-d), second, u_pair["up" if d == 1 else "down"], ypair)
        push(slot(-d), second_half[d], u_far, xdev(d))
    reduce_step(2, True)
    arrived(m.act.at[slot(0, True), first], g_pair)
    for d in (1, -1):
        push(slot(0, True), first, g_near[1, d], xdev(d))
    reduce_step(2, False)
    ring2.hop(0, 3)
    ring2.hop(1, 2)
    attention_step(2)
    weight_grad(rep, (first, second), m.xt, True)
    for key, (r, _) in near.items():
        arrived(m.yt.at[r, own_half], near_sems[key])
        remote(m.yt.at[r, own_half], m.yt.at[r, own_half], near_sib_sem, sib)
    reduce_step(3, True)
    reduce_step(3, False)
    attention_step(3)
    ring2.hop(0, 4)
    ring2.hop(1, 3)
    for d in (1, -1):
        arrived(m.act.at[slot(-d), first], g_near[0, d])
        push(slot(-d), first_half[d], g_far[0], xdev(d))
    arrived(m.yt.at[pl.ds(0, 3), own_half], near_sib_sem)
    weight_grad(slot(1), (first, second))
    weight_grad(slot(-1), (first, second))
    arrived(m.act.at[slot(2), second], u_far)
    push(slot(2), second, u_pair["far"], ypair)
    reduce_step(4, True)
    attention_step(4)
    weight_grad(slot(0, True), (first,))
    for d in (1, -1):
        arrived(m.act.at[slot(-d, True), first], g_near[1, d])
        push(slot(-d, True), first_half[d], g_far[1], xdev(d))
    ring2.hop(1, 4)

    out, _, total = merged([m.am[z], earlier(-1, 4), earlier(1, 3)])
    m.att[tail] = out / total
    att_sem = sem()
    remote(m.att.at[tail], m.att.at[tail], att_sem, yhi)

    need(0)
    value = jnp.concatenate(
        [own_term(0, c) + taken(-1, c, chain[-1, c]) + taken(1, c, chain[1, c]) for c in (0, 1)], axis=0
    )
    m.fin[...] = value.T.reshape(4, ROWS, HALF)
    m.fsend[0] = m.fin[far_quarter].astype(BF16)
    m.fsend[1] = m.fin[(1 - core) * 2 + other].astype(BF16)
    y_sem, diagonal_sem, fsib_sem = sem(), sem(), sem()
    remote(m.fsend.at[0], m.frecv.at[0], y_sem, yhi)
    remote(m.fsend.at[1], m.frecv.at[1], diagonal_sem, diagonal)
    remote(m.fin.at[(1 - core) * 2 + tail], m.fsib, fsib_sem, sib)

    for o in (0, -1, 1, -2, 2, -3, 3, 4):
        ring2.rest(o)
    weight_grad(slot(2), (second,))
    for d in (1, -1):
        weight_grad(slot(-d, True), (first,))

    arrived(m.act.at[slot(0, True), second], u_pair["own"])
    weight_grad(slot(0, True), (second,))
    for d in (1, -1):
        arrived(m.act.at[slot(-d, True), second], u_pair["up" if d == 1 else "down"])
        weight_grad(slot(-d, True), (second,))

    stores = []
    for s in (0, 1):
        arrived(m.act.at[slot(2, s == 1), first], g_far[s])
        weight_grad(slot(2, s == 1), (first,))

    def store(i, out_ref):
        part = pl.ds(i * HID, HID)
        m.og[part] = (m.dw[part] * SCALE).astype(BF16)
        stores.append(load(m.og.at[part], out_ref, small_sems[2 + i]))

    store(0, m.gg_out)
    arrived(m.act.at[slot(2, True), second], u_pair["far"])
    weight_grad(slot(2, True), (second,))
    store(1, m.gu_out)

    arrived(m.att.at[other], att_sem)
    for s in range(2):
        owner0 = m.owners[(rep * 2 + s) * 2]
        owner1 = m.owners[(rep * 2 + s) * 2 + 1]
        for hp in range(2):
            cols = slice(hp * HD, (hp + 1) * HD)
            a = m.att[s, hp * 4 : hp * 4 + 2]
            b = m.att[s, hp * 4 + 2 : hp * 4 + 4]
            none = jnp.zeros_like(a)
            b = jnp.where(owner1 == tail, b, none)
            m.at[s * 2, :, cols] = jnp.where(owner0 == tail, a, b).astype(BF16)
            m.at[s * 2 + 1, :, cols] = jnp.where(owner0 == tail, b, none).astype(BF16)
    stores.append(load(m.at, m.at_out, small_sems[0]))

    arrived(m.fsib, fsib_sem)
    arrived(m.frecv.at[0], y_sem)
    arrived(m.frecv.at[1], diagonal_sem)
    mine = pl.ds(pl.multiple_of(core * HALF, HALF), HALF)
    theirs = pl.ds(pl.multiple_of((1 - core) * HALF, HALF), HALF)
    m.ig[:, mine] = (m.fin[quarter] + m.frecv[0].astype(F32)).astype(BF16)
    m.ig[:, theirs] = (m.fsib[...] + m.frecv[1].astype(F32)).astype(BF16)
    stores.append(load(m.ig, m.ig_out, small_sems[1]))

    for copy in outgoing[-SENDS:] + outgoing_large:
        copy.wait_send()
    for copy in stores:
        copy.wait()
    assert used[0] == N_SEMS, used[0]


def hand_on(*refs):
    ins, outs, bufs, sems = refs[:4], refs[4:8], refs[8:12], refs[12]
    loads = [pltpu.make_async_copy(ins[i], bufs[i], sems.at[i]) for i in range(4)]
    stores = [pltpu.make_async_copy(bufs[i], outs[i], sems.at[i]) for i in range(4)]
    for load in loads:
        load.start()
    for load, store in zip(loads, stores):
        load.wait()
        store.start()
    for store in stores:
        store.wait()


def per_device(
    tokens, w_gate, w_up, hidden_grad, kv_pool, block_table, tail_len, tail_owner, new_queries, new_kv
):
    hbm = pl.BlockSpec(memory_space=pl.ANY)
    out_shape = (
        jax.ShapeDtypeStruct((ROWS, TOK), BF16),
        jax.ShapeDtypeStruct((HID, PLANE), BF16),
        jax.ShapeDtypeStruct((HID, PLANE), BF16),
        jax.ShapeDtypeStruct((4, 2, 2 * HD), BF16),
    )
    results = pl.pallas_call(
        kernel,
        out_shape=out_shape,
        in_specs=[hbm] * 10,
        out_specs=(hbm,) * 4,
        scratch_shapes=list(SCRATCH.values()),
        compiler_params=pltpu.CompilerParams(
            collective_id=0, has_side_effects=True, vmem_limit_bytes=60 * 2**20
        ),
        cost_estimate=pl.CostEstimate(flops=6_300_000_000, bytes_accessed=12_000_000, transcendentals=300_000),
    )(
        tokens.T.reshape(2, ROWS // 2, TOK),
        w_gate.T,
        w_up.T,
        hidden_grad.T,
        kv_pool.reshape(POS, 1024),
        new_queries,
        new_kv,
        block_table,
        tail_len,
        tail_owner.reshape(-1),
    )
    input_grad, grad_gate, grad_up, attn = pl.pallas_call(
        hand_on,
        out_shape=out_shape,
        in_specs=[hbm] * 4,
        out_specs=(hbm,) * 4,
        scratch_shapes=[pltpu.VMEM(out.shape, out.dtype) for out in out_shape]
        + [pltpu.SemaphoreType.DMA((4,))],
    )(*results)
    return input_grad.T, grad_gate.T, grad_up.T, attn


def solution(mesh):
    in_specs = (
        P("rep", ("tp", "tail")),
        P(None, ("tp", "tail")),
        P(None, ("tp", "tail")),
        P("rep", ("tp", "tail")),
        P(("rep", "tp", "tail"), None, None),
        P(("rep", "tail"), "tp"),
        P(),
        P(),
        P(("rep", "tail"), None, None),
        P(("rep", "tail"), None, None),
    )
    out_specs = (
        P("rep", ("tp", "tail")),
        P("rep", ("tp", "tail")),
        P("rep", ("tp", "tail")),
        P(("rep", "tail"), None, "tp"),
    )
    return jax.shard_map(
        per_device, mesh=mesh, in_specs=in_specs, out_specs=out_specs, check_vma=False
    )
```

```python
import functools

import jax
import jax.numpy as jnp
from jax import lax
from jax.experimental import pallas as pl
from jax.experimental.pallas import tpu as pltpu
from jax.sharding import PartitionSpec as P

NR = 8
NZ = 8
NX = 4
ROWS = 160
TOK = 256
PLANE = 4 * ROWS
HALF = TOK // 2
PART = TOK // 4
HID = 400
ACTS = 2 * HID
CUT = 448
KVH = 4
HD = 128
CPD = 256
POS = 512
MASK_VALUE = -1e30
SCALE = 2048 ** (-0.5)
F32 = jnp.float32
BF16 = jnp.bfloat16
NT = (((1,), (1,)), ((), ()))
MESH = pl.DeviceIdType.MESH
SENDS = 24
N_SEMS = 160

SCRATCH = dict(
    xt=pltpu.VMEM((NZ, 4, 2, ROWS // 2, TOK), BF16),
    yt=pltpu.VMEM((NR, 4, 2, ROWS // 2, TOK), BF16),
    w=pltpu.VMEM((NZ, ACTS, PLANE), BF16),
    hgrad=pltpu.VMEM((HID, TOK), BF16),
    h=pltpu.VMEM((ACTS, TOK), F32),
    act=pltpu.VMEM((NR, ACTS, TOK), BF16),
    tact=pltpu.VMEM((2, 2, HALF, HID), BF16),
    pf=pltpu.VMEM((NZ, 2, PART, PLANE), F32),
    ss=pltpu.VMEM((NZ, 2, PART, PLANE), BF16),
    sb=pltpu.VMEM((NZ, 2, PART, PLANE), BF16),
    rs=pltpu.VMEM((14, PART, PLANE), BF16),
    rb=pltpu.VMEM((14, PART, PLANE), BF16),
    fin=pltpu.VMEM((4, ROWS, HALF), F32),
    fsend=pltpu.VMEM((2, ROWS, HALF), BF16),
    fsib=pltpu.VMEM((ROWS, HALF), F32),
    frecv=pltpu.VMEM((2, ROWS, HALF), BF16),
    dw=pltpu.VMEM((ACTS, PLANE), F32),
    kv=pltpu.VMEM((POS, 1024), BF16),
    q=pltpu.VMEM((2, 2, 4096), BF16),
    nkv=pltpu.VMEM((2, 2, 1024), BF16),
    qs=pltpu.VMEM((KVH, 32, HD), F32),
    kf=pltpu.VMEM((16, 1024), F32),
    ao=pltpu.VMEM((2, NZ, 16, HD), F32),
    asib=pltpu.VMEM((NZ, 16, HD), F32),
    am=pltpu.VMEM((NZ, 16, HD), F32),
    asend=pltpu.VMEM((7, 16, HD), F32),
    ar=pltpu.VMEM((7, 16, HD), F32),
    att=pltpu.VMEM((2, 8, HD), F32),
    ig=pltpu.VMEM((ROWS, TOK), BF16),
    og=pltpu.VMEM((ACTS, PLANE), BF16),
    at=pltpu.VMEM((4, 2, 2 * HD), BF16),
    table=pltpu.SMEM((2, 16), jnp.int32),
    lens=pltpu.SMEM((32,), jnp.int32),
    owners=pltpu.SMEM((32,), jnp.int32),
    met=pltpu.SemaphoreType.REGULAR((2,)),
    sems=pltpu.SemaphoreType.DMA((N_SEMS,)),
)
INPUTS = ("tok_in", "wg_in", "wu_in", "hgrad_in", "kv_in", "q_in", "nkv_in", "table_in", "lens_in", "owners_in")
OUTPUTS = ("ig_out", "gg_out", "gu_out", "at_out")


class Refs:
    def __init__(self, names, refs):
        for name, ref in zip(names, refs):
            setattr(self, name, ref)


def kernel(*refs):
    m = Refs(INPUTS + OUTPUTS + tuple(SCRATCH), refs)
    rep = lax.axis_index("rep")
    tp = lax.axis_index("tp")
    tail = lax.axis_index("tail")
    x, ylo = rep // 2, rep % 2
    z, core = tp // 2, tp % 2
    other = 1 - tail
    quarter, far_quarter = core * 2 + tail, core * 2 + other

    sib = {"tp": z * 2 + (1 - core)}
    yhi = {"tail": other}
    diagonal = {"tp": z * 2 + (1 - core), "tail": other}
    ypair = {"rep": x * 2 + (1 - ylo)}

    def zdev(d):
        return {"tp": lax.rem(z + d + NZ, NZ) * 2 + core}

    def xdev(d):
        return {"rep": lax.rem(x + d + NX, NX) * 2 + ylo}

    def gone(like, sent):
        pltpu.make_async_remote_copy(
            src_ref=like, dst_ref=like, send_sem=sent, recv_sem=sent, device_id=sib, device_id_type=MESH
        ).wait_send()

    def plane_at(o):
        return lax.rem(z + o + NZ, NZ)

    def slot(o, pair=False):
        return lax.rem(x + o + NX, NX) * 2 + ((1 - ylo) if pair else ylo)

    def far(f, back=False):
        dx = jnp.where(f < 2, 2, jnp.where((f == 2) != back, 1, 3))
        return lax.rem(x + dx, NX) * 2 + jnp.where(f == 0, ylo, 1 - ylo)

    used = [0]

    def sem(count=1):
        first = used[0]
        used[0] += count
        return m.sems.at[first] if count == 1 else first

    outgoing = []
    first_send = sem(SENDS)

    def remote(src, dst, recv, dev):
        place = len(outgoing)
        if place >= SENDS:
            outgoing[place - SENDS].wait_send()
        copy = pltpu.make_async_remote_copy(
            src_ref=src,
            dst_ref=dst,
            send_sem=m.sems.at[first_send + place % SENDS],
            recv_sem=recv,
            device_id=dev,
            device_id_type=MESH,
        )
        copy.start()
        outgoing.append(copy)

    def arrived(dst, recv):
        pltpu.make_async_remote_copy(
            src_ref=dst, dst_ref=dst, send_sem=recv, recv_sem=recv, device_id=sib, device_id_type=MESH
        ).wait_recv()

    barrier = pltpu.get_barrier_semaphore()

    def greet(dev, on=barrier):
        pl.semaphore_signal(on, inc=1, device_id=dev, device_id_type=MESH)

    target, source = far(z // 2, True), far(z // 2)
    peers = [zdev(1), zdev(-1), sib, yhi, ypair, xdev(1), xdev(-1)]
    for dev in peers:
        greet(dev)

    def load(src, dst, on=None):
        copy = pltpu.make_async_copy(src, dst, sem() if on is None else on)
        copy.start()
        return copy

    tok_load = load(m.tok_in, m.xt.at[z, quarter])
    class Ring:
        def __init__(self, place, pieces, across):
            self.place = place
            self.pieces = range(pieces)
            self.across = across
            hops = {(0, 0): 3, (0, 1): 3, (1, 0): 3, (1, 1): 2 if across else 3}
            self.last_hop = {(d, s, u): hops[s, u] for d in (1, -1) for s in (0, 1) for u in self.pieces}
            self.last_hop[1, 0, 0] = 4
            self.last_hop[(-1, 0, 1) if across else (-1, 1, 0)] = 4
            self.recv = [[[sem() for _ in self.pieces] for _ in range(2)] for _ in range(NZ)]
            self.from_sib = [sem() for _ in range(NZ)]

        def piece(self, o, s, u=None):
            return self.place(plane_at(o), quarter if s == 0 else far_quarter, u)

        def to_sib(self, o, s):
            remote(self.piece(o, s), self.piece(o, s), self.from_sib[o % NZ], sib)

        def along(self, o, s, u, d):
            remote(self.piece(o, s, u), self.piece(o, s, u), self.recv[(o - d) % NZ][s][u], zdev(d))

        def exchange(self, o, u):
            remote(self.piece(o, 0, u), self.piece(o, 0, u), self.recv[o % NZ][1][u], yhi)

        def taken(self, o, s, u):
            arrived(self.piece(o, s, u), self.recv[o % NZ][s][u])

        def start(self, s):
            for u in self.pieces:
                if s == 1:
                    self.taken(0, 1, u)
                for d in (1, -1):
                    self.along(0, s, u, d)
            self.to_sib(0, s)

        def hop(self, s, h):
            whole = []
            for u in self.pieces:
                for d in (1, -1):
                    o = -d * h
                    if h <= self.last_hop[d, s, u]:
                        self.taken(o, s, u)
                        if h < self.last_hop[d, s, u]:
                            self.along(o, s, u, d)
                        if self.across and s == 0 and h + u >= 4:
                            self.exchange(o, u)
                        if u == self.pieces[-1]:
                            whole.append(o)
            for o in whole:
                self.to_sib(o, s)

        def crossed(self, o):
            for u in self.pieces:
                if o == 4 or u == 1:
                    self.taken(o, 1, u)
            self.to_sib(o, 1)

        def rest(self, o):
            both = self.place(plane_at(o), pl.ds((1 - core) * 2, 2), None)
            arrived(both, self.from_sib[o % NZ])

    ring = Ring(lambda plane, q, u: m.xt.at[plane, q] if u is None else m.xt.at[plane, q, u], 2, True)
    ring2 = Ring(lambda plane, q, u: m.yt.at[far(plane // 2), q, plane % 2], 1, False)

    tok_load.wait()
    pl.semaphore_wait(barrier, len(peers))

    for u in (0, 1):
        ring.exchange(0, u)
        for d in (1, -1):
            ring.along(0, 0, u, d)
    ring.to_sib(0, 0)

    small_sems = [sem() for _ in range(6)]
    small_loads = [
        load(m.table_in, m.table, small_sems[0]),
        load(m.lens_in, m.lens, small_sems[1]),
        load(m.owners_in, m.owners, small_sems[2]),
        load(m.q_in, m.q, small_sems[3]),
        load(m.nkv_in, m.nkv, small_sems[4]),
        load(m.kv_in, m.kv, small_sems[5]),
    ]
    w_loads = {}
    for o in (0, -1, 1, -2, 2, -3, 3, 4):
        plane = plane_at(o)
        cols = pl.ds(pl.multiple_of(plane * PLANE, 128), PLANE)
        w_sem = sem()
        load(m.wg_in.at[:, cols], m.w.at[plane, pl.ds(0, HID)], w_sem)
        load(m.wu_in.at[:, cols], m.w.at[plane, pl.ds(HID, HID)], w_sem)
        w_loads[o] = pltpu.make_async_copy(m.w.at[plane], m.w.at[plane], w_sem)
    hgrad_load = load(m.hgrad_in, m.hgrad)

    first_sem = sem()
    own_half = pl.ds(core * 2, 2)
    near = {"pair": (slot(0, True), ypair), 1: (slot(1), xdev(1)), -1: (slot(-1), xdev(-1))}
    near_sems = {key: sem() for key in near}
    near_sib_sem = sem()

    near_sent, seed_sent = sem(), sem()

    def later(src, dst, sent, recv, dev):
        return pltpu.make_async_remote_copy(
            src_ref=src, dst_ref=dst, send_sem=sent, recv_sem=recv, device_id=dev, device_id_type=MESH
        )

    leaving = {(s, pair): [] for s in (0, 1) for pair in (False, True)}
    piece = m.yt.at[rep, quarter, z % 2]
    seed = later(m.xt.at[target, quarter, z % 2], piece, seed_sent, first_sem, {"rep": target})
    leaving[0, False].append((target, seed))
    for s, q in ((0, quarter), (1, far_quarter)):
        for key, (r, dev) in near.items():
            to = near_sems[key if key == "pair" else -key]
            leaving[s, key == "pair"].append((r, later(m.xt.at[r, q], m.yt.at[rep, q], near_sent, to, dev)))

    def leave(s, pair, *hops):
        for r, copy in leaving[s, pair]:
            away = lax.rem(r - z + NZ, NZ)
            now = functools.reduce(jnp.logical_or, [(away == h) | (away == NZ - h) for h in hops])
            pl.when(now)(copy.start)

    def project(o):
        w_loads[o].wait()
        ring.rest(o)
        plane = plane_at(o)
        for part in (pl.ds(0, HID), pl.ds(HID, HID)):
            value = jnp.dot(m.w[plane, part], m.xt[plane].reshape(PLANE, TOK), preferred_element_type=F32)
            if o == 0:
                m.h[part] = value
            else:
                m.h[part] += value

    def merged(parts):
        tops = [part[8:16, 0:1] for part in parts]
        top = functools.reduce(jnp.maximum, tops)
        scaling = [jnp.exp(t - top) for t in tops]
        out = sum(scale * part[0:8] for scale, part in zip(scaling, parts))
        total = sum(scale * part[8:16, HD // 2 : HD // 2 + 1] for scale, part in zip(scaling, parts))
        return out, top, total

    for copy in small_loads:
        copy.wait()
    m.kf[...] = jnp.zeros_like(m.kf)
    for n in range(2):
        m.kf[n * 2 : n * 2 + 2, :] = m.nkv[n].astype(F32)
        for head in range(32):
            g, q = head // 8, head % 8
            m.qs[g, q * 4 + n * 2 : q * 4 + n * 2 + 2, :] = m.q[n, :, head * HD : (head + 1) * HD].astype(F32)
    lane = lax.broadcasted_iota(jnp.int32, (8, POS), 1)
    row_tail = lax.broadcasted_iota(jnp.int32, (8, POS), 0) // 2 % 2
    page, offset = lane // 16, lane % 16
    places = []
    for n in range(2):
        place = jnp.full((8, POS), 1 << 20, jnp.int32)
        for b in range(16):
            place = jnp.where(page == m.table[n, b], tp * CPD + b * 16 + offset, place)
        places.append(place)
    home = rep * 2 + tail
    limit = jnp.where(row_tail == 0, m.lens[home * 2], m.lens[home * 2 + 1])
    live = (jnp.where(row_tail == 0, places[0], places[1]) < limit).astype(jnp.int32)
    live = jnp.concatenate([live] * 4, axis=0) > 0
    f_row = lax.broadcasted_iota(jnp.int32, (32, 16), 0)
    f_col = lax.broadcasted_iota(jnp.int32, (32, 16), 1)
    f_live = (f_col // 2 == f_row // 2 % 2) & (f_col % 2 <= f_row % 2) & (f_col + 16 * tp < 4)
    low_lanes = lax.broadcasted_iota(jnp.int32, (8, HD), 1) < HD // 2

    def both(top, total):
        return jnp.where(low_lanes, top, total)

    for g in range(KVH):
        cols, vcols = slice(g * HD, (g + 1) * HD), slice((KVH + g) * HD, (KVH + g + 1) * HD)
        q = m.qs[g].astype(BF16)
        s = lax.dot_general(q, m.kv[:, cols], NT, preferred_element_type=F32) * HD ** (-0.5)
        fs = lax.dot_general(q, m.kf[:, cols].astype(BF16), NT, preferred_element_type=F32) * HD ** (-0.5)
        s, fs = jnp.where(live, s, MASK_VALUE), jnp.where(f_live, fs, MASK_VALUE)
        top = jnp.maximum(jnp.max(s, axis=1, keepdims=True), jnp.max(fs, axis=1, keepdims=True))
        p = jnp.where(live, jnp.exp(s - top), 0.0)
        fp = jnp.where(f_live, jnp.exp(fs - top), 0.0)
        total = jnp.sum(p, axis=1, keepdims=True) + jnp.sum(fp, axis=1, keepdims=True)
        out = jnp.dot(p.astype(BF16), m.kv[:, vcols], preferred_element_type=F32) + jnp.dot(
            fp.astype(BF16), m.kf[:, vcols].astype(BF16), preferred_element_type=F32
        )
        for j in range(4):
            rows = slice(j * 8, j * 8 + 8)
            to = g * 4 + j
            m.ao[to % 2, to // 2, 0:8] = out[rows]
            m.ao[to % 2, to // 2, 8:16] = both(top[rows], total[rows])

    asib_sem = sem()
    remote(m.ao.at[1 - core], m.asib, asib_sem, sib)
    ar_sems = [sem() for _ in range(7)]

    def earlier(d, i):
        place = i - 1 if d == -1 else 3 + i
        arrived(m.ar.at[place], ar_sems[place])
        return m.ar[place]

    def attention_step(i):
        for d, length in ((-1, 4), (1, 3)):
            if i <= length:
                place = i - 1 if d == -1 else 3 + i
                dest = plane_at(d * (length - i + 1))
                if i == 1:
                    m.asend[place] = m.am[dest]
                else:
                    out, top, total = merged([m.am[dest], earlier(d, i - 1)])
                    m.asend[place, 0:8] = out
                    m.asend[place, 8:16] = both(top, total)
                remote(m.asend.at[place], m.ar.at[place], ar_sems[place], zdev(d))

    for dev in (sib, yhi, ypair, xdev(1), xdev(-1)):
        greet(dev, m.met.at[0])
    ring.hop(0, 1)
    ring.start(1)
    pl.semaphore_wait(m.met.at[0], 5)
    greet(ypair, m.met.at[1])
    ring.hop(0, 2)
    pl.semaphore_wait(m.met.at[1], 1)
    leave(0, False, 0, 1, 2)
    leave(0, True, 0, 1, 2)
    ring.hop(1, 1)
    project(0)
    leave(1, False, 0, 1)
    leave(1, True, 0, 1)
    ring.hop(0, 3)
    leave(0, False, 3)
    ring.hop(1, 2)
    leave(1, False, 2)
    leave(1, True, 2)

    arrived(m.asib, asib_sem)
    for i in range(NZ):
        out, top, total = merged([m.ao[core, i], m.asib[i]])
        m.am[i, 0:8] = out
        m.am[i, 8:16] = both(top, total)

    ring.hop(0, 4)
    leave(0, False, 4)
    project(-1)
    project(1)
    ring.hop(1, 3)
    ring.crossed(-3)
    ring.crossed(3)
    leave(1, False, 3)
    attention_step(1)
    project(-2)
    project(2)
    arrived(ring2.piece(0, 0), first_sem)
    ring2.exchange(0, 0)
    ring2.start(0)
    ring.crossed(4)
    leave(1, False, 4)
    for s in (0, 1):
        leave(s, True, 3, 4)
    project(-3)
    project(3)
    project(4)

    hgrad_load.wait()
    gate, up = m.h[0:HID], m.h[HID:ACTS]
    sg = jax.nn.sigmoid(gate)
    grad_out = m.hgrad[...].astype(F32)
    act_gate = grad_out * up * sg * (1.0 + gate * (1.0 - sg))
    act_up = grad_out * gate * sg
    m.act[rep, 0:HID] = act_gate.astype(BF16)
    m.act[rep, HID:ACTS] = act_up.astype(BF16)

    first, second = pl.ds(0, CUT), pl.ds(CUT, ACTS - CUT)
    first_half = {1: pl.ds(0, CUT // 2), -1: pl.ds(CUT // 2, CUT // 2)}
    second_half = {1: pl.ds(CUT, (ACTS - CUT) // 2), -1: pl.ds((CUT + ACTS) // 2, (ACTS - CUT) // 2)}

    act_sent = sem()

    def push(s, part, recv, dev):
        ref = m.act.at[s, part]
        later(ref, ref, act_sent, recv, dev).start()

    g_pair = sem()
    g_near = {(s, d): sem() for s in (0, 1) for d in (1, -1)}
    g_far = {s: sem() for s in (0, 1)}
    u_near = {d: sem() for d in (1, -1)}
    u_far = sem()
    u_pair = {key: sem() for key in ("own", "up", "down", "far")}

    push(rep, first, g_pair, ypair)
    for d in (1, -1):
        push(rep, second, u_near[d], xdev(d))

    for i, value in enumerate((act_gate, act_up)):
        for half in (0, 1):
            m.tact[i, lax.rem(half + core, 2)] = value[:, half * HALF : (half + 1) * HALF].T.astype(BF16)


    sb_sems = [sem() for _ in range(NZ)]

    def partial(o):
        plane = plane_at(o)
        value = sum(
            jnp.dot(m.tact[i].reshape(TOK, HID), m.w[plane, pl.ds(i * HID, HID)], preferred_element_type=F32)
            for i in (0, 1)
        )
        m.pf[plane] = value[:HALF].reshape(2, PART, PLANE)
        m.ss[plane] = value[HALF:].reshape(2, PART, PLANE).astype(BF16)
        remote(m.ss.at[plane], m.sb.at[plane], sb_sems[o % NZ], sib)

    chain = {(-1, 0): 4, (-1, 1): 3, (1, 0): 3, (1, 1): 4}
    places_of, count = {}, 0
    for key, length in chain.items():
        for i in range(1, length + 1):
            places_of[key + (i,)] = count
            count += 1
    rb_sems = [sem() for _ in range(count)]

    def own_term(o, c):
        plane = plane_at(o)
        return m.pf[plane, c] + m.sb[plane, c].astype(F32)

    def taken(d, c, i):
        place = places_of[d, c, i]
        arrived(m.rb.at[place], rb_sems[place])
        return m.rb[place].astype(F32)

    ready = set()

    def need(o):
        if o % NZ not in ready:
            ready.add(o % NZ)
            arrived(m.sb.at[plane_at(o)], sb_sems[o % NZ])

    def reduce_step(i, longer):
        for d, c in ((-1, 0), (1, 1)) if longer else ((-1, 1), (1, 0)):
            o = d * (chain[d, c] - i + 1)
            need(o)
            value = own_term(o, c)
            if i > 1:
                value += taken(d, c, i - 1)
            place = places_of[d, c, i]
            m.rs[place] = value.astype(BF16)
            remote(m.rs.at[place], m.rb.at[place], rb_sems[place], zdev(d))

    def weight_grad(slots, parts, tokens=None, fresh=False):
        buf = m.yt if tokens is None else tokens
        rows = jnp.concatenate([buf[s].reshape(PLANE, TOK) for s in slots], axis=1)
        for part in parts:
            acts = jnp.concatenate([m.act[s, part] for s in slots], axis=1)
            value = lax.dot_general(acts, rows, NT, preferred_element_type=F32)
            if fresh:
                m.dw[part] = value
            else:
                m.dw[part] += value

    ring2.hop(0, 1)
    ring2.start(1)
    partial(4)
    attention_step(2)
    partial(-3)
    partial(3)
    reduce_step(1, True)
    partial(-2)
    reduce_step(1, False)
    ring2.hop(0, 2)
    partial(2)
    for d in (1, -1):
        push(rep, first, g_near[0, d], xdev(d))
    partial(-1)
    partial(1)
    push(rep, second, u_pair["own"], ypair)
    attention_step(3)
    ring2.hop(1, 1)
    partial(0)
    for d in (1, -1):
        arrived(m.act.at[slot(-d), second], u_near[d])
        push(slot(-d), second, u_pair["up" if d == 1 else "down"], ypair)
        push(slot(-d), second_half[d], u_far, xdev(d))
    reduce_step(2, True)
    arrived(m.act.at[slot(0, True), first], g_pair)
    for d in (1, -1):
        push(slot(0, True), first, g_near[1, d], xdev(d))
    reduce_step(2, False)
    ring2.hop(0, 3)
    ring2.hop(1, 2)
    attention_step(4)
    weight_grad((rep,), (first, second), m.xt, True)
    for key, (r, _) in near.items():
        arrived(m.yt.at[r, own_half], near_sems[key])
        remote(m.yt.at[r, own_half], m.yt.at[r, own_half], near_sib_sem, sib)
    reduce_step(3, True)
    reduce_step(3, False)
    ring2.hop(0, 4)
    ring2.hop(1, 3)
    for d in (1, -1):
        arrived(m.act.at[slot(-d), first], g_near[0, d])
        push(slot(-d), first_half[d], g_far[0], xdev(d))
    arrived(m.yt.at[pl.ds(0, 3), own_half], near_sib_sem)
    weight_grad((slot(1), slot(-1)), (first, second))
    arrived(m.act.at[slot(2), second], u_far)
    push(slot(2), second, u_pair["far"], ypair)
    reduce_step(4, True)
    out, _, total = merged([m.am[z], earlier(-1, 4), earlier(1, 3)])
    m.att[tail] = out / total
    att_sem = sem()
    remote(m.att.at[tail], m.att.at[tail], att_sem, yhi)
    for d in (1, -1):
        arrived(m.act.at[slot(-d, True), first], g_near[1, d])
        push(slot(-d, True), first_half[d], g_far[1], xdev(d))
    ring2.hop(1, 4)

    need(0)
    value = jnp.concatenate(
        [own_term(0, c) + taken(-1, c, chain[-1, c]) + taken(1, c, chain[1, c]) for c in (0, 1)], axis=0
    )
    m.fin[...] = value.T.reshape(4, ROWS, HALF)
    m.fsend[0] = m.fin[far_quarter].astype(BF16)
    m.fsend[1] = m.fin[(1 - core) * 2 + other].astype(BF16)
    y_sem, diagonal_sem, fsib_sem = sem(), sem(), sem()
    remote(m.fsend.at[0], m.frecv.at[0], y_sem, yhi)
    remote(m.fsend.at[1], m.frecv.at[1], diagonal_sem, diagonal)
    remote(m.fin.at[(1 - core) * 2 + tail], m.fsib, fsib_sem, sib)

    for o in (0, -1, 1, -2, 2, -3, 3, 4):
        ring2.rest(o)
    weight_grad((slot(1, True), slot(-1, True)), (first,))
    arrived(m.act.at[slot(0, True), second], u_pair["own"])
    weight_grad((slot(0, True), slot(2)), (second,))
    for d in (1, -1):
        arrived(m.act.at[slot(-d, True), second], u_pair["up" if d == 1 else "down"])
    weight_grad((slot(1, True), slot(-1, True)), (second,))
    stores = []

    arrived(m.act.at[slot(2), first], g_far[0])
    weight_grad((slot(0, True), slot(2)), (first,))
    arrived(m.act.at[slot(2, True), first], g_far[1])
    weight_grad((slot(2, True),), (first,))

    def store(i, out_ref):
        part = pl.ds(i * HID, HID)
        m.og[part] = (m.dw[part] * SCALE).astype(BF16)
        stores.append(load(m.og.at[part], out_ref, small_sems[2 + i]))

    store(0, m.gg_out)
    arrived(m.act.at[slot(2, True), second], u_pair["far"])
    weight_grad((slot(2, True),), (second,))
    store(1, m.gu_out)

    arrived(m.att.at[other], att_sem)
    for s in range(2):
        owner0 = m.owners[(rep * 2 + s) * 2]
        owner1 = m.owners[(rep * 2 + s) * 2 + 1]
        for hp in range(2):
            cols = slice(hp * HD, (hp + 1) * HD)
            a = m.att[s, hp * 4 : hp * 4 + 2]
            b = m.att[s, hp * 4 + 2 : hp * 4 + 4]
            none = jnp.zeros_like(a)
            b = jnp.where(owner1 == tail, b, none)
            m.at[s * 2, :, cols] = jnp.where(owner0 == tail, a, b).astype(BF16)
            m.at[s * 2 + 1, :, cols] = jnp.where(owner0 == tail, b, none).astype(BF16)
    stores.append(load(m.at, m.at_out, small_sems[0]))

    arrived(m.fsib, fsib_sem)
    arrived(m.frecv.at[0], y_sem)
    arrived(m.frecv.at[1], diagonal_sem)
    mine = pl.ds(pl.multiple_of(core * HALF, HALF), HALF)
    theirs = pl.ds(pl.multiple_of((1 - core) * HALF, HALF), HALF)
    m.ig[:, mine] = (m.fin[quarter] + m.frecv[0].astype(F32)).astype(BF16)
    m.ig[:, theirs] = (m.fsib[...] + m.frecv[1].astype(F32)).astype(BF16)
    stores.append(load(m.ig, m.ig_out, small_sems[1]))

    for copy in outgoing[-SENDS:]:
        copy.wait_send()
    seed.wait_send()
    gone(m.xt.at[pl.ds(0, 3), pl.ds(0, 2)], near_sent)
    gone(m.act.at[pl.ds(0, 7)], act_sent)
    for copy in stores:
        copy.wait()
    assert used[0] == N_SEMS, used[0]


def hand_on(*refs):
    ins, outs, bufs, sems = refs[:4], refs[4:8], refs[8:12], refs[12]
    loads = [pltpu.make_async_copy(ins[i], bufs[i], sems.at[i]) for i in range(4)]
    stores = [pltpu.make_async_copy(bufs[i], outs[i], sems.at[i]) for i in range(4)]
    for load in loads:
        load.start()
    for load, store in zip(loads, stores):
        load.wait()
        store.start()
    for store in stores:
        store.wait()


def per_device(
    tokens, w_gate, w_up, hidden_grad, kv_pool, block_table, tail_len, tail_owner, new_queries, new_kv
):
    hbm = pl.BlockSpec(memory_space=pl.ANY)
    out_shape = (
        jax.ShapeDtypeStruct((ROWS, TOK), BF16),
        jax.ShapeDtypeStruct((HID, PLANE), BF16),
        jax.ShapeDtypeStruct((HID, PLANE), BF16),
        jax.ShapeDtypeStruct((4, 2, 2 * HD), BF16),
    )
    results = pl.pallas_call(
        kernel,
        out_shape=out_shape,
        in_specs=[hbm] * 10,
        out_specs=(hbm,) * 4,
        scratch_shapes=list(SCRATCH.values()),
        compiler_params=pltpu.CompilerParams(
            collective_id=0, has_side_effects=True, vmem_limit_bytes=60 * 2**20
        ),
        cost_estimate=pl.CostEstimate(flops=6_300_000_000, bytes_accessed=12_000_000, transcendentals=300_000),
    )(
        tokens.T.reshape(2, ROWS // 2, TOK),
        w_gate.T,
        w_up.T,
        hidden_grad.T,
        kv_pool.reshape(POS, 1024),
        new_queries,
        new_kv,
        block_table,
        tail_len,
        tail_owner.reshape(-1),
    )
    input_grad, grad_gate, grad_up, attn = pl.pallas_call(
        hand_on,
        out_shape=out_shape,
        in_specs=[hbm] * 4,
        out_specs=(hbm,) * 4,
        scratch_shapes=[pltpu.VMEM(out.shape, out.dtype) for out in out_shape]
        + [pltpu.SemaphoreType.DMA((4,))],
    )(*results)
    return input_grad.T, grad_gate.T, grad_up.T, attn


def solution(mesh):
    in_specs = (
        P("rep", ("tp", "tail")),
        P(None, ("tp", "tail")),
        P(None, ("tp", "tail")),
        P("rep", ("tp", "tail")),
        P(("rep", "tp", "tail"), None, None),
        P(("rep", "tail"), "tp"),
        P(),
        P(),
        P(("rep", "tail"), None, None),
        P(("rep", "tail"), None, None),
    )
    out_specs = (
        P("rep", ("tp", "tail")),
        P("rep", ("tp", "tail")),
        P("rep", ("tp", "tail")),
        P(("rep", "tail"), None, "tp"),
    )
    return jax.shard_map(
        per_device, mesh=mesh, in_specs=in_specs, out_specs=out_specs, check_vma=False
    )
```

```python
import functools

import jax
import jax.numpy as jnp
from jax import lax
from jax.experimental import pallas as pl
from jax.experimental.pallas import tpu as pltpu
from jax.sharding import PartitionSpec as P

NR = 8
NZ = 8
NX = 4
ROWS = 160
TOK = 256
PLANE = 4 * ROWS
HALF = TOK // 2
PART = TOK // 4
HID = 400
ACTS = 2 * HID
CUT = 448
KVH = 4
HD = 128
CPD = 256
POS = 512
MASK_VALUE = -1e30
SCALE = 2048 ** (-0.5)
F32 = jnp.float32
BF16 = jnp.bfloat16
NT = (((1,), (1,)), ((), ()))
MESH = pl.DeviceIdType.MESH
SENDS = 24
N_SEMS = 160

SCRATCH = dict(
    xt=pltpu.VMEM((NZ, 4, 2, ROWS // 2, TOK), BF16),
    yt=pltpu.VMEM((NR, 4, 2, ROWS // 2, TOK), BF16),
    w=pltpu.VMEM((NZ, ACTS, PLANE), BF16),
    hgrad=pltpu.VMEM((HID, TOK), BF16),
    h=pltpu.VMEM((ACTS, TOK), F32),
    act=pltpu.VMEM((NR, ACTS, TOK), BF16),
    tact=pltpu.VMEM((2, 2, HALF, HID), BF16),
    pf=pltpu.VMEM((NZ, 2, PART, PLANE), F32),
    ss=pltpu.VMEM((NZ, 2, PART, PLANE), BF16),
    sb=pltpu.VMEM((NZ, 2, PART, PLANE), BF16),
    rs=pltpu.VMEM((14, PART, PLANE), BF16),
    rb=pltpu.VMEM((14, PART, PLANE), BF16),
    fin=pltpu.VMEM((4, ROWS, HALF), F32),
    fsend=pltpu.VMEM((2, ROWS, HALF), BF16),
    fsib=pltpu.VMEM((ROWS, HALF), F32),
    frecv=pltpu.VMEM((2, ROWS, HALF), BF16),
    dw=pltpu.VMEM((ACTS, PLANE), F32),
    kv=pltpu.VMEM((POS, 1024), BF16),
    q=pltpu.VMEM((2, 2, 4096), BF16),
    nkv=pltpu.VMEM((2, 2, 1024), BF16),
    qs=pltpu.VMEM((KVH, 32, HD), F32),
    kf=pltpu.VMEM((16, 1024), F32),
    ao=pltpu.VMEM((2, NZ, 16, HD), F32),
    asib=pltpu.VMEM((NZ, 16, HD), F32),
    am=pltpu.VMEM((NZ, 16, HD), F32),
    asend=pltpu.VMEM((7, 16, HD), F32),
    ar=pltpu.VMEM((7, 16, HD), F32),
    att=pltpu.VMEM((2, 8, HD), F32),
    ig=pltpu.VMEM((ROWS, TOK), BF16),
    og=pltpu.VMEM((ACTS, PLANE), BF16),
    at=pltpu.VMEM((4, 2, 2 * HD), BF16),
    table=pltpu.SMEM((2, 16), jnp.int32),
    lens=pltpu.SMEM((32,), jnp.int32),
    owners=pltpu.SMEM((32,), jnp.int32),
    met=pltpu.SemaphoreType.REGULAR((2,)),
    sems=pltpu.SemaphoreType.DMA((N_SEMS,)),
)
INPUTS = ("tok_in", "wg_in", "wu_in", "hgrad_in", "kv_in", "q_in", "nkv_in", "table_in", "lens_in", "owners_in")
OUTPUTS = ("ig_out", "gg_out", "gu_out", "at_out")


class Refs:
    def __init__(self, names, refs):
        for name, ref in zip(names, refs):
            setattr(self, name, ref)


def kernel(*refs):
    m = Refs(INPUTS + OUTPUTS + tuple(SCRATCH), refs)
    rep = lax.axis_index("rep")
    tp = lax.axis_index("tp")
    tail = lax.axis_index("tail")
    x, ylo = rep // 2, rep % 2
    z, core = tp // 2, tp % 2
    other = 1 - tail
    quarter, far_quarter = core * 2 + tail, core * 2 + other

    sib = {"tp": z * 2 + (1 - core)}
    yhi = {"tail": other}
    diagonal = {"tp": z * 2 + (1 - core), "tail": other}
    ypair = {"rep": x * 2 + (1 - ylo)}

    def zdev(d):
        return {"tp": lax.rem(z + d + NZ, NZ) * 2 + core}

    def xdev(d):
        return {"rep": lax.rem(x + d + NX, NX) * 2 + ylo}

    def gone(like, sent):
        pltpu.make_async_remote_copy(
            src_ref=like, dst_ref=like, send_sem=sent, recv_sem=sent, device_id=sib, device_id_type=MESH
        ).wait_send()

    def plane_at(o):
        return lax.rem(z + o + NZ, NZ)

    def slot(o, pair=False):
        return lax.rem(x + o + NX, NX) * 2 + ((1 - ylo) if pair else ylo)

    def far(f, back=False):
        dx = jnp.where(f < 2, 2, jnp.where((f == 2) != back, 1, 3))
        return lax.rem(x + dx, NX) * 2 + jnp.where(f == 0, ylo, 1 - ylo)

    used = [0]

    def sem(count=1):
        first = used[0]
        used[0] += count
        return m.sems.at[first] if count == 1 else first

    outgoing = []
    first_send = sem(SENDS)

    def remote(src, dst, recv, dev):
        place = len(outgoing)
        if place >= SENDS:
            outgoing[place - SENDS].wait_send()
        copy = pltpu.make_async_remote_copy(
            src_ref=src,
            dst_ref=dst,
            send_sem=m.sems.at[first_send + place % SENDS],
            recv_sem=recv,
            device_id=dev,
            device_id_type=MESH,
        )
        copy.start()
        outgoing.append(copy)

    def arrived(dst, recv):
        pltpu.make_async_remote_copy(
            src_ref=dst, dst_ref=dst, send_sem=recv, recv_sem=recv, device_id=sib, device_id_type=MESH
        ).wait_recv()

    barrier = pltpu.get_barrier_semaphore()

    def greet(dev, on=barrier):
        pl.semaphore_signal(on, inc=1, device_id=dev, device_id_type=MESH)

    target, source = far(z // 2, True), far(z // 2)
    peers = [zdev(1), zdev(-1), sib, yhi, ypair, xdev(1), xdev(-1)]
    for dev in peers:
        greet(dev)

    def load(src, dst, on=None):
        copy = pltpu.make_async_copy(src, dst, sem() if on is None else on)
        copy.start()
        return copy

    tok_load = load(m.tok_in, m.xt.at[z, quarter])
    class Ring:
        def __init__(self, place, pieces, across):
            self.place = place
            self.pieces = range(pieces)
            self.across = across
            hops = {(0, 0): 3, (0, 1): 3, (1, 0): 3, (1, 1): 2 if across else 3}
            self.last_hop = {(d, s, u): hops[s, u] for d in (1, -1) for s in (0, 1) for u in self.pieces}
            self.last_hop[1, 0, 0] = 4
            self.last_hop[(-1, 0, 1) if across else (-1, 1, 0)] = 4
            self.recv = [[[sem() for _ in self.pieces] for _ in range(2)] for _ in range(NZ)]
            self.from_sib = [sem() for _ in range(NZ)]

        def piece(self, o, s, u=None):
            return self.place(plane_at(o), quarter if s == 0 else far_quarter, u)

        def to_sib(self, o, s):
            remote(self.piece(o, s), self.piece(o, s), self.from_sib[o % NZ], sib)

        def along(self, o, s, u, d):
            remote(self.piece(o, s, u), self.piece(o, s, u), self.recv[(o - d) % NZ][s][u], zdev(d))

        def exchange(self, o, u):
            remote(self.piece(o, 0, u), self.piece(o, 0, u), self.recv[o % NZ][1][u], yhi)

        def taken(self, o, s, u):
            arrived(self.piece(o, s, u), self.recv[o % NZ][s][u])

        def start(self, s):
            for u in self.pieces:
                if s == 1:
                    self.taken(0, 1, u)
                for d in (1, -1):
                    self.along(0, s, u, d)
            self.to_sib(0, s)

        def hop(self, s, h):
            whole = []
            for u in self.pieces:
                for d in (1, -1):
                    o = -d * h
                    if h <= self.last_hop[d, s, u]:
                        self.taken(o, s, u)
                        if h < self.last_hop[d, s, u]:
                            self.along(o, s, u, d)
                        if self.across and s == 0 and h + u >= 4:
                            self.exchange(o, u)
                        if u == self.pieces[-1]:
                            whole.append(o)
            for o in whole:
                self.to_sib(o, s)

        def crossed(self, o):
            for u in self.pieces:
                if o == 4 or u == 1:
                    self.taken(o, 1, u)
            self.to_sib(o, 1)

        def rest(self, o):
            both = self.place(plane_at(o), pl.ds((1 - core) * 2, 2), None)
            arrived(both, self.from_sib[o % NZ])

    ring = Ring(lambda plane, q, u: m.xt.at[plane, q] if u is None else m.xt.at[plane, q, u], 2, True)
    ring2 = Ring(lambda plane, q, u: m.yt.at[far(plane // 2), q, plane % 2], 1, False)

    tok_load.wait()
    pl.semaphore_wait(barrier, len(peers))

    for u in (0, 1):
        ring.exchange(0, u)
        for d in (1, -1):
            ring.along(0, 0, u, d)
    ring.to_sib(0, 0)

    small_sems = [sem() for _ in range(6)]
    small_loads = [
        load(m.table_in, m.table, small_sems[0]),
        load(m.lens_in, m.lens, small_sems[1]),
        load(m.owners_in, m.owners, small_sems[2]),
        load(m.q_in, m.q, small_sems[3]),
        load(m.nkv_in, m.nkv, small_sems[4]),
        load(m.kv_in, m.kv, small_sems[5]),
    ]
    w_loads = {}
    for o in (0, -1, 1, -2, 2, -3, 3, 4):
        plane = plane_at(o)
        cols = pl.ds(pl.multiple_of(plane * PLANE, 128), PLANE)
        w_sem = sem()
        load(m.wg_in.at[:, cols], m.w.at[plane, pl.ds(0, HID)], w_sem)
        load(m.wu_in.at[:, cols], m.w.at[plane, pl.ds(HID, HID)], w_sem)
        w_loads[o] = pltpu.make_async_copy(m.w.at[plane], m.w.at[plane], w_sem)
    hgrad_load = load(m.hgrad_in, m.hgrad)

    first_sem = sem()
    own_half = pl.ds(core * 2, 2)
    near = {"pair": (slot(0, True), ypair), 1: (slot(1), xdev(1)), -1: (slot(-1), xdev(-1))}
    near_sems = {key: sem() for key in near}
    near_sib_sem = sem()

    near_sent, seed_sent = sem(), sem()

    def later(src, dst, sent, recv, dev):
        return pltpu.make_async_remote_copy(
            src_ref=src, dst_ref=dst, send_sem=sent, recv_sem=recv, device_id=dev, device_id_type=MESH
        )

    leaving = {(s, pair): [] for s in (0, 1) for pair in (False, True)}
    piece = m.yt.at[rep, quarter, z % 2]
    seed = later(m.xt.at[target, quarter, z % 2], piece, seed_sent, first_sem, {"rep": target})
    leaving[0, False].append((target, seed))
    for s, q in ((0, quarter), (1, far_quarter)):
        for key, (r, dev) in near.items():
            to = near_sems[key if key == "pair" else -key]
            leaving[s, key == "pair"].append((r, later(m.xt.at[r, q], m.yt.at[rep, q], near_sent, to, dev)))

    def leave(s, pair, *hops):
        for r, copy in leaving[s, pair]:
            away = lax.rem(r - z + NZ, NZ)
            now = functools.reduce(jnp.logical_or, [(away == h) | (away == NZ - h) for h in hops])
            pl.when(now)(copy.start)

    def project(o):
        w_loads[o].wait()
        ring.rest(o)
        plane = plane_at(o)
        for part in (pl.ds(0, HID), pl.ds(HID, HID)):
            value = jnp.dot(m.w[plane, part], m.xt[plane].reshape(PLANE, TOK), preferred_element_type=F32)
            if o == 0:
                m.h[part] = value
            else:
                m.h[part] += value

    def merged(parts):
        tops = [part[8:16, 0:1] for part in parts]
        top = functools.reduce(jnp.maximum, tops)
        scaling = [jnp.exp(t - top) for t in tops]
        out = sum(scale * part[0:8] for scale, part in zip(scaling, parts))
        total = sum(scale * part[8:16, HD // 2 : HD // 2 + 1] for scale, part in zip(scaling, parts))
        return out, top, total

    for copy in small_loads:
        copy.wait()
    m.kf[...] = jnp.zeros_like(m.kf)
    for n in range(2):
        m.kf[n * 2 : n * 2 + 2, :] = m.nkv[n].astype(F32)
        for head in range(32):
            g, q = head // 8, head % 8
            m.qs[g, q * 4 + n * 2 : q * 4 + n * 2 + 2, :] = m.q[n, :, head * HD : (head + 1) * HD].astype(F32)
    lane = lax.broadcasted_iota(jnp.int32, (8, POS), 1)
    row_tail = lax.broadcasted_iota(jnp.int32, (8, POS), 0) // 2 % 2
    page, offset = lane // 16, lane % 16
    places = []
    for n in range(2):
        place = jnp.full((8, POS), 1 << 20, jnp.int32)
        for b in range(16):
            place = jnp.where(page == m.table[n, b], tp * CPD + b * 16 + offset, place)
        places.append(place)
    home = rep * 2 + tail
    limit = jnp.where(row_tail == 0, m.lens[home * 2], m.lens[home * 2 + 1])
    live = (jnp.where(row_tail == 0, places[0], places[1]) < limit).astype(jnp.int32)
    live = jnp.concatenate([live] * 4, axis=0) > 0
    f_row = lax.broadcasted_iota(jnp.int32, (32, 16), 0)
    f_col = lax.broadcasted_iota(jnp.int32, (32, 16), 1)
    f_live = (f_col // 2 == f_row // 2 % 2) & (f_col % 2 <= f_row % 2) & (f_col + 16 * tp < 4)
    low_lanes = lax.broadcasted_iota(jnp.int32, (8, HD), 1) < HD // 2

    def both(top, total):
        return jnp.where(low_lanes, top, total)

    for g in range(KVH):
        cols, vcols = slice(g * HD, (g + 1) * HD), slice((KVH + g) * HD, (KVH + g + 1) * HD)
        q = m.qs[g].astype(BF16)
        s = lax.dot_general(q, m.kv[:, cols], NT, preferred_element_type=F32) * HD ** (-0.5)
        fs = lax.dot_general(q, m.kf[:, cols].astype(BF16), NT, preferred_element_type=F32) * HD ** (-0.5)
        s, fs = jnp.where(live, s, MASK_VALUE), jnp.where(f_live, fs, MASK_VALUE)
        top = jnp.maximum(jnp.max(s, axis=1, keepdims=True), jnp.max(fs, axis=1, keepdims=True))
        p = jnp.where(live, jnp.exp(s - top), 0.0)
        fp = jnp.where(f_live, jnp.exp(fs - top), 0.0)
        total = jnp.sum(p, axis=1, keepdims=True) + jnp.sum(fp, axis=1, keepdims=True)
        out = jnp.dot(p.astype(BF16), m.kv[:, vcols], preferred_element_type=F32) + jnp.dot(
            fp.astype(BF16), m.kf[:, vcols].astype(BF16), preferred_element_type=F32
        )
        for j in range(4):
            rows = slice(j * 8, j * 8 + 8)
            to = g * 4 + j
            m.ao[to % 2, to // 2, 0:8] = out[rows]
            m.ao[to % 2, to // 2, 8:16] = both(top[rows], total[rows])

    asib_sem = sem()
    remote(m.ao.at[1 - core], m.asib, asib_sem, sib)
    ar_sems = [sem() for _ in range(7)]

    def earlier(d, i):
        place = i - 1 if d == -1 else 3 + i
        arrived(m.ar.at[place], ar_sems[place])
        return m.ar[place]

    def attention_step(i):
        for d, length in ((-1, 4), (1, 3)):
            if i <= length:
                place = i - 1 if d == -1 else 3 + i
                dest = plane_at(d * (length - i + 1))
                if i == 1:
                    m.asend[place] = m.am[dest]
                else:
                    out, top, total = merged([m.am[dest], earlier(d, i - 1)])
                    m.asend[place, 0:8] = out
                    m.asend[place, 8:16] = both(top, total)
                remote(m.asend.at[place], m.ar.at[place], ar_sems[place], zdev(d))

    for dev in (sib, yhi, ypair, xdev(1), xdev(-1)):
        greet(dev, m.met.at[0])
    ring.hop(0, 1)
    ring.start(1)
    pl.semaphore_wait(m.met.at[0], 5)
    greet(ypair, m.met.at[1])
    ring.hop(0, 2)
    pl.semaphore_wait(m.met.at[1], 1)
    leave(0, False, 0, 1, 2)
    leave(0, True, 0, 1, 2)
    ring.hop(1, 1)
    project(0)
    leave(1, False, 0, 1)
    leave(1, True, 0, 1)
    ring.hop(0, 3)
    leave(0, False, 3)
    ring.hop(1, 2)
    leave(1, False, 2)
    leave(1, True, 2)

    arrived(m.asib, asib_sem)
    for i in range(NZ):
        out, top, total = merged([m.ao[core, i], m.asib[i]])
        m.am[i, 0:8] = out
        m.am[i, 8:16] = both(top, total)

    ring.hop(0, 4)
    leave(0, False, 4)
    project(-1)
    project(1)
    ring.hop(1, 3)
    ring.crossed(-3)
    ring.crossed(3)
    leave(1, False, 3)
    attention_step(1)
    project(-2)
    project(2)
    arrived(ring2.piece(0, 0), first_sem)
    ring2.exchange(0, 0)
    ring2.start(0)
    ring.crossed(4)
    leave(1, False, 4)
    for s in (0, 1):
        leave(s, True, 3, 4)
    project(-3)
    project(3)
    project(4)

    hgrad_load.wait()
    gate, up = m.h[0:HID], m.h[HID:ACTS]
    sg = jax.nn.sigmoid(gate)
    grad_out = m.hgrad[...].astype(F32)
    act_gate = grad_out * up * sg * (1.0 + gate * (1.0 - sg))
    act_up = grad_out * gate * sg
    m.act[rep, 0:HID] = act_gate.astype(BF16)
    m.act[rep, HID:ACTS] = act_up.astype(BF16)

    first, second = pl.ds(0, CUT), pl.ds(CUT, ACTS - CUT)
    first_half = {1: pl.ds(0, CUT // 2), -1: pl.ds(CUT // 2, CUT // 2)}
    second_half = {1: pl.ds(CUT, (ACTS - CUT) // 2), -1: pl.ds((CUT + ACTS) // 2, (ACTS - CUT) // 2)}

    act_sent = sem()

    def push(s, part, recv, dev):
        ref = m.act.at[s, part]
        later(ref, ref, act_sent, recv, dev).start()

    g_pair = sem()
    g_near = {(s, d): sem() for s in (0, 1) for d in (1, -1)}
    g_far = {s: sem() for s in (0, 1)}
    u_near = {d: sem() for d in (1, -1)}
    u_far = sem()
    u_pair = {key: sem() for key in ("own", "up", "down", "far")}

    push(rep, first, g_pair, ypair)
    for d in (1, -1):
        push(rep, second, u_near[d], xdev(d))

    for i, value in enumerate((act_gate, act_up)):
        for half in (0, 1):
            m.tact[i, lax.rem(half + core, 2)] = value[:, half * HALF : (half + 1) * HALF].T.astype(BF16)


    sb_sems = [sem() for _ in range(NZ)]

    def partial(o):
        plane = plane_at(o)
        value = sum(
            jnp.dot(m.tact[i].reshape(TOK, HID), m.w[plane, pl.ds(i * HID, HID)], preferred_element_type=F32)
            for i in (0, 1)
        )
        m.pf[plane] = value[:HALF].reshape(2, PART, PLANE)
        m.ss[plane] = value[HALF:].reshape(2, PART, PLANE).astype(BF16)
        remote(m.ss.at[plane], m.sb.at[plane], sb_sems[o % NZ], sib)

    chain = {(-1, 0): 4, (-1, 1): 3, (1, 0): 3, (1, 1): 4}
    places_of, count = {}, 0
    for key, length in chain.items():
        for i in range(1, length + 1):
            places_of[key + (i,)] = count
            count += 1
    rb_sems = [sem() for _ in range(count)]

    def own_term(o, c):
        plane = plane_at(o)
        return m.pf[plane, c] + m.sb[plane, c].astype(F32)

    def taken(d, c, i):
        place = places_of[d, c, i]
        arrived(m.rb.at[place], rb_sems[place])
        return m.rb[place].astype(F32)

    ready = set()

    def need(o):
        if o % NZ not in ready:
            ready.add(o % NZ)
            arrived(m.sb.at[plane_at(o)], sb_sems[o % NZ])

    def reduce_step(i, longer):
        for d, c in ((-1, 0), (1, 1)) if longer else ((-1, 1), (1, 0)):
            o = d * (chain[d, c] - i + 1)
            need(o)
            value = own_term(o, c)
            if i > 1:
                value += taken(d, c, i - 1)
            place = places_of[d, c, i]
            m.rs[place] = value.astype(BF16)
            remote(m.rs.at[place], m.rb.at[place], rb_sems[place], zdev(d))

    def weight_grad(slots, parts, tokens=None, fresh=False):
        buf = m.yt if tokens is None else tokens
        rows = jnp.concatenate([buf[s].reshape(PLANE, TOK) for s in slots], axis=1)
        for part in parts:
            acts = jnp.concatenate([m.act[s, part] for s in slots], axis=1)
            value = lax.dot_general(acts, rows, NT, preferred_element_type=F32)
            if fresh:
                m.dw[part] = value
            else:
                m.dw[part] += value

    ring2.hop(0, 1)
    ring2.start(1)
    partial(4)
    attention_step(2)
    partial(-3)
    partial(3)
    reduce_step(1, True)
    partial(-2)
    reduce_step(1, False)
    ring2.hop(0, 2)
    partial(2)
    for d in (1, -1):
        push(rep, first, g_near[0, d], xdev(d))
    partial(-1)
    partial(1)
    push(rep, second, u_pair["own"], ypair)
    attention_step(3)
    ring2.hop(1, 1)
    for d in (1, -1):
        arrived(m.act.at[slot(-d), second], u_near[d])
        push(slot(-d), second, u_pair["up" if d == 1 else "down"], ypair)
        push(slot(-d), second_half[d], u_far, xdev(d))
    partial(0)
    reduce_step(2, True)
    arrived(m.act.at[slot(0, True), first], g_pair)
    for d in (1, -1):
        push(slot(0, True), first, g_near[1, d], xdev(d))
    reduce_step(2, False)
    ring2.hop(0, 3)
    ring2.hop(1, 2)
    attention_step(4)
    weight_grad((rep,), (first, second), m.xt, True)
    for key, (r, _) in near.items():
        arrived(m.yt.at[r, own_half], near_sems[key])
        remote(m.yt.at[r, own_half], m.yt.at[r, own_half], near_sib_sem, sib)
    reduce_step(3, True)
    reduce_step(3, False)
    ring2.hop(0, 4)
    ring2.hop(1, 3)
    for d in (1, -1):
        arrived(m.act.at[slot(-d), first], g_near[0, d])
        push(slot(-d), first_half[d], g_far[0], xdev(d))
    arrived(m.yt.at[pl.ds(0, 3), own_half], near_sib_sem)
    weight_grad((slot(1), slot(-1)), (first, second))
    arrived(m.act.at[slot(2), second], u_far)
    push(slot(2), second, u_pair["far"], ypair)
    reduce_step(4, True)
    arrived(m.act.at[slot(0, True), second], u_pair["own"])
    weight_grad((slot(0, True),), (first, second))
    out, _, total = merged([m.am[z], earlier(-1, 4), earlier(1, 3)])
    m.att[tail] = out / total
    att_sem = sem()
    remote(m.att.at[tail], m.att.at[tail], att_sem, yhi)
    for d in (1, -1):
        arrived(m.act.at[slot(-d, True), first], g_near[1, d])
        push(slot(-d, True), first_half[d], g_far[1], xdev(d))
    ring2.hop(1, 4)

    need(0)
    value = jnp.concatenate(
        [own_term(0, c) + taken(-1, c, chain[-1, c]) + taken(1, c, chain[1, c]) for c in (0, 1)], axis=0
    )
    m.fin[...] = value.T.reshape(4, ROWS, HALF)
    m.fsend[0] = m.fin[far_quarter].astype(BF16)
    m.fsend[1] = m.fin[(1 - core) * 2 + other].astype(BF16)
    y_sem, diagonal_sem, fsib_sem = sem(), sem(), sem()
    remote(m.fsend.at[0], m.frecv.at[0], y_sem, yhi)
    remote(m.fsend.at[1], m.frecv.at[1], diagonal_sem, diagonal)
    remote(m.fin.at[(1 - core) * 2 + tail], m.fsib, fsib_sem, sib)

    for o in (0, -1, 1, -2, 2, -3, 3, 4):
        ring2.rest(o)
    weight_grad((slot(1, True), slot(-1, True)), (first,))
    for d in (1, -1):
        arrived(m.act.at[slot(-d, True), second], u_pair["up" if d == 1 else "down"])
    weight_grad((slot(1, True), slot(-1, True)), (second,))
    stores = []

    arrived(m.act.at[slot(2, True), second], u_pair["far"])
    weight_grad((slot(2), slot(2, True)), (second,))
    for s in (0, 1):
        arrived(m.act.at[slot(2, s == 1), first], g_far[s])
    weight_grad((slot(2), slot(2, True)), (first,))

    def store(i, out_ref):
        part = pl.ds(i * HID, HID)
        m.og[part] = (m.dw[part] * SCALE).astype(BF16)
        stores.append(load(m.og.at[part], out_ref, small_sems[2 + i]))

    store(0, m.gg_out)
    store(1, m.gu_out)

    arrived(m.att.at[other], att_sem)
    for s in range(2):
        owner0 = m.owners[(rep * 2 + s) * 2]
        owner1 = m.owners[(rep * 2 + s) * 2 + 1]
        for hp in range(2):
            cols = slice(hp * HD, (hp + 1) * HD)
            a = m.att[s, hp * 4 : hp * 4 + 2]
            b = m.att[s, hp * 4 + 2 : hp * 4 + 4]
            none = jnp.zeros_like(a)
            b = jnp.where(owner1 == tail, b, none)
            m.at[s * 2, :, cols] = jnp.where(owner0 == tail, a, b).astype(BF16)
            m.at[s * 2 + 1, :, cols] = jnp.where(owner0 == tail, b, none).astype(BF16)
    stores.append(load(m.at, m.at_out, small_sems[0]))

    arrived(m.fsib, fsib_sem)
    arrived(m.frecv.at[0], y_sem)
    arrived(m.frecv.at[1], diagonal_sem)
    mine = pl.ds(pl.multiple_of(core * HALF, HALF), HALF)
    theirs = pl.ds(pl.multiple_of((1 - core) * HALF, HALF), HALF)
    m.ig[:, mine] = (m.fin[quarter] + m.frecv[0].astype(F32)).astype(BF16)
    m.ig[:, theirs] = (m.fsib[...] + m.frecv[1].astype(F32)).astype(BF16)
    stores.append(load(m.ig, m.ig_out, small_sems[1]))

    for copy in outgoing[-SENDS:]:
        copy.wait_send()
    seed.wait_send()
    gone(m.xt.at[pl.ds(0, 3), pl.ds(0, 2)], near_sent)
    gone(m.act.at[pl.ds(0, 7)], act_sent)
    for copy in stores:
        copy.wait()
    assert used[0] == N_SEMS, used[0]


def hand_on(*refs):
    ins, outs, bufs, sems = refs[:4], refs[4:8], refs[8:12], refs[12]
    loads = [pltpu.make_async_copy(ins[i], bufs[i], sems.at[i]) for i in range(4)]
    stores = [pltpu.make_async_copy(bufs[i], outs[i], sems.at[i]) for i in range(4)]
    for load in loads:
        load.start()
    for load, store in zip(loads, stores):
        load.wait()
        store.start()
    for store in stores:
        store.wait()


def per_device(
    tokens, w_gate, w_up, hidden_grad, kv_pool, block_table, tail_len, tail_owner, new_queries, new_kv
):
    hbm = pl.BlockSpec(memory_space=pl.ANY)
    out_shape = (
        jax.ShapeDtypeStruct((ROWS, TOK), BF16),
        jax.ShapeDtypeStruct((HID, PLANE), BF16),
        jax.ShapeDtypeStruct((HID, PLANE), BF16),
        jax.ShapeDtypeStruct((4, 2, 2 * HD), BF16),
    )
    results = pl.pallas_call(
        kernel,
        out_shape=out_shape,
        in_specs=[hbm] * 10,
        out_specs=(hbm,) * 4,
        scratch_shapes=list(SCRATCH.values()),
        compiler_params=pltpu.CompilerParams(
            collective_id=0, has_side_effects=True, vmem_limit_bytes=60 * 2**20
        ),
        cost_estimate=pl.CostEstimate(flops=6_300_000_000, bytes_accessed=12_000_000, transcendentals=300_000),
    )(
        tokens.T.reshape(2, ROWS // 2, TOK),
        w_gate.T,
        w_up.T,
        hidden_grad.T,
        kv_pool.reshape(POS, 1024),
        new_queries,
        new_kv,
        block_table,
        tail_len,
        tail_owner.reshape(-1),
    )
    input_grad, grad_gate, grad_up, attn = pl.pallas_call(
        hand_on,
        out_shape=out_shape,
        in_specs=[hbm] * 4,
        out_specs=(hbm,) * 4,
        scratch_shapes=[pltpu.VMEM(out.shape, out.dtype) for out in out_shape]
        + [pltpu.SemaphoreType.DMA((4,))],
    )(*results)
    return input_grad.T, grad_gate.T, grad_up.T, attn


def solution(mesh):
    in_specs = (
        P("rep", ("tp", "tail")),
        P(None, ("tp", "tail")),
        P(None, ("tp", "tail")),
        P("rep", ("tp", "tail")),
        P(("rep", "tp", "tail"), None, None),
        P(("rep", "tail"), "tp"),
        P(),
        P(),
        P(("rep", "tail"), None, None),
        P(("rep", "tail"), None, None),
    )
    out_specs = (
        P("rep", ("tp", "tail")),
        P("rep", ("tp", "tail")),
        P("rep", ("tp", "tail")),
        P(("rep", "tail"), None, "tp"),
    )
    return jax.shard_map(
        per_device, mesh=mesh, in_specs=in_specs, out_specs=out_specs, check_vma=False
    )
```
